32 devices in a mesh: section: 4 (over z), expert: 8 (over y, x, core).
Axes of the slice: x: 2, y: 2, z: 4, core: 2. Of those that a mesh axis runs over, the one named last changes fastest.
Arguments:
- tokens: bfloat16 [10240, 768], P(('section', 'expert')), may hold values from -6 to 6
- gate_prob: float32 [10240], P(('section', 'expert')), may hold values from 0.1 to 1
- routing: int32 [10240, 1], P(('section', 'expert')), may hold values from 0 to 7; in each aligned block of 320 rows (0 to 319, 320 to 639, ...) at most 80 rows name the same one
- up_weight: bfloat16 [32, 768, 512], P(('section', 'expert')), may hold values from -0.21875 to 0.21875
- down_weight: bfloat16 [32, 512, 768], P(('section', 'expert')), may hold values from -0.1875 to 0.1875
- cotangent: bfloat16 [10240, 768], P(('section', 'expert')), may hold values from -6 to 6
Outputs:
- mixed: bfloat16 [10240, 768], P(('section', 'expert'))
- token_grad: bfloat16 [10240, 768], P(('section', 'expert'))
- grad_up: bfloat16 [32, 768, 512], P(('section', 'expert'))
- grad_down: bfloat16 [32, 512, 768], P(('section', 'expert'))
The draws below stay inside these ranges and needn't reach their ends.
Inputs may be any that keep to these rules, and one draw needn't show every extreme that they name: `routing`: at most 80 of one device's 320 tokens name the same expert, and in every draw some device's tokens name one expert exactly 80 times.
All inputs are finite; a program needn't handle non-finite values.
Results may differ from the reference program's by a relative error of at most 0.0065.
Values may be sent and summed in bfloat16 or wider, within the bound.
No kernel may reach another device: no remote copies, remote signals or barrier semaphores. Data moves between devices by JAX's collectives and lax.ppermute only.
A program may use at most 64 MiB of HBM per device.

```python
import math
import jax
import jax.numpy as jnp
import numpy as np
from jax import lax

D = 768
FF = 1024
TOK_DEV = 320
EXPERTS = 16
CAP = 80
TOKENS = 10240
N_SECTION = 4
N_EXPERT = 8


def levels(key, shape, cuts, least, largest):
    factor_of, own = 1.0, jax.random.fold_in(key, 6)
    for dim, shards_of in cuts:
        draws = jnp.exp(jax.random.uniform(jax.random.fold_in(own, dim), (shards_of,), jnp.float32, least / len(cuts), largest / len(cuts)))
        factor_of = factor_of * jnp.repeat(draws, shape[dim] // shards_of).reshape([-1 if axis == dim else 1 for axis in range(len(shape))])
    return factor_of


def routed_block(key, own, number, rows, amount, top, most, lean):
    order = jax.random.permutation(key, amount)
    heavy_load, common = portions_of(amount, rows * top, most, lean, True), portions_of(amount, rows * top, most, lean, False)
    places = jnp.arange(amount)

    def named(tallies, rotation):
        used = int((tallies > 0).sum())
        fixed = max(1, used // 4)
        moved = fixed + (places - fixed + rotation * (used - fixed)) % max(1, amount - fixed)
        return jnp.zeros((amount,), jnp.int32).at[order[jnp.where(places < fixed, places, moved)]].set(jnp.asarray(tallies, jnp.int32))

    tallies = jnp.where(number % 4 == 0, named(heavy_load, number // 4), named(common, number - number // 4 - 1))
    mixed = jax.random.permutation(jax.random.fold_in(own, 3), amount)
    source_of, taker = mixed[0:amount // 2 * 2:2], mixed[1:amount // 2 * 2:2]
    slack = jnp.minimum(tallies[source_of] - 1, most - tallies[taker]) // 2
    slack = jnp.where((source_of == order[0]) | (taker == order[0]) | (tallies[taker] == 0), 0, jnp.maximum(slack, 0))
    moved = jax.random.randint(jax.random.fold_in(own, 4), (amount // 2,), 0, 1 << 20) % (slack + 1)
    tallies = tallies.at[source_of].add(-moved).at[taker].add(moved)
    labels = jnp.searchsorted(jnp.cumsum(tallies), jnp.arange(rows * top), side="right").astype(jnp.int32)
    grid = labels.reshape(top, rows).T
    grid = grid[jax.random.permutation(jax.random.fold_in(own, 1), rows)]
    rotation = jax.random.randint(jax.random.fold_in(own, 2), (rows, 1), 0, top)
    return jnp.take_along_axis(grid, (jnp.arange(top)[None, :] + rotation) % top, axis=1)


def portions_of(amount, total, limit, slope, full):
    portions = [(1 << 20) // math.isqrt(grade ** slope) + 1 for grade in range(1, amount + 1)]
    largest = limit if full else min(limit, max(-(-total // amount), total * portions[0] // sum(portions)))
    least = 1 if total - largest >= amount - 1 else 0
    given, rest = [largest] + [least] * (amount - 1), total - largest - least * (amount - 1)
    while rest > 0:
        free = [i for i in range(1, amount) if given[i] < largest] or [i for i in range(1, amount) if given[i] < limit]
        whole, budget = sum([portions[i] for i in free]), rest
        for i in free:
            extra = min(limit - given[i], max(1, budget * portions[i] // whole), rest)
            given[i] = given[i] + extra
            rest = rest - extra
    return np.array(given)


def scatter_about(key, shape, deviation, limit, split=(), kind=jnp.bfloat16):
    level = levels(key, shape, split, -0.22, 0.18) if split else 1.0
    array = jax.random.normal(key, shape, jnp.float32) * deviation * level
    return jnp.minimum(jnp.maximum(array, -limit), limit).astype(kind)


def setup_inputs(seed: int = 0) -> dict:
    key_list = jax.random.split(jax.random.key(seed), 7)
    tokens = scatter_about(key_list[0], (TOKENS, D), 1.0, 6.0, ((0, 32),))
    gate_prob = jnp.clip(0.1 + 0.9 * jax.random.uniform(key_list[1], (TOKENS,), jnp.float32) ** levels(key_list[1], (TOKENS,), ((0, 32),), -0.2, 0.2), 0.1, 1.0)
    routing_keys = jax.random.split(jax.random.fold_in(key_list[2], 1), TOKENS // TOK_DEV)
    routing_turns = jax.random.permutation(jax.random.fold_in(key_list[2], 3), TOKENS // TOK_DEV)
    routing = jax.vmap(lambda own, number: routed_block(jax.random.fold_in(key_list[2], 2), own, number, TOK_DEV, N_EXPERT, 1, CAP, 2))(routing_keys, routing_turns).reshape((TOKENS, 1))
    up_weight = scatter_about(key_list[3], (2 * EXPERTS, D, FF // 2), D ** -0.5, 0.21875, ((0, 32),))
    down_weight = scatter_about(key_list[4], (2 * EXPERTS, FF // 2, D), FF ** -0.5, 0.1875, ((0, 32),))
    cotangent = scatter_about(key_list[5], (TOKENS, D), 1.0, 6.0, ((0, 32),))
    return {"tokens": tokens, "gate_prob": gate_prob, "routing": routing, "up_weight": up_weight, "down_weight": down_weight, "cotangent": cotangent}


def gelu_value(preact):
    inner = 0.7978845608 * (preact + 0.044715 * preact * preact * preact)
    return 0.5 * preact * (1.0 + jnp.tanh(inner))


def gelu_slope(preact):
    inner = 0.7978845608 * (preact + 0.044715 * preact * preact * preact)
    tangent = jnp.tanh(inner)
    return 0.5 * (1.0 + tangent) + 0.5 * preact * (1.0 - tangent * tangent) * 0.7978845608 * (1.0 + 0.134145 * preact * preact)


def slot_positions(route_col, experts, capacity):
    choose = (route_col == jnp.arange(experts, dtype=jnp.int32)[None, :]).astype(jnp.int32)
    running = jnp.cumsum(choose, axis=0)
    ranking = jnp.sum(running * choose, axis=1) - 1
    return (route_col[:, 0] * capacity + ranking).astype(jnp.int32)


def expert_pass(inputs):
    token_rows, grad_rows, w_up, w_down = inputs
    preact = jnp.dot(token_rows, w_up, preferred_element_type=jnp.float32)
    hidden = gelu_value(preact).astype(jnp.bfloat16)
    output_rows = jnp.dot(hidden, w_down, preferred_element_type=jnp.float32).astype(jnp.bfloat16)
    through = jnp.dot(grad_rows, w_down.T, preferred_element_type=jnp.float32)
    hidden_grad = (through * gelu_slope(preact)).astype(jnp.bfloat16)
    input_grad = jnp.dot(hidden_grad, w_up.T, preferred_element_type=jnp.float32).astype(jnp.bfloat16)
    grad_up = jnp.dot(token_rows.T, hidden_grad, preferred_element_type=jnp.float32).astype(jnp.bfloat16)
    grad_down = jnp.dot(hidden.T, grad_rows, preferred_element_type=jnp.float32).astype(jnp.bfloat16)
    return output_rows, input_grad, grad_up, grad_down


def group_pass(inputs):
    return lax.map(expert_pass, inputs)


def reference(tokens, gate_prob, routing, up_weight, down_weight, cotangent):
    groups = N_SECTION // 2
    half_ff = FF // 2
    slot_count = N_EXPERT * CAP
    scaled = (gate_prob[:, None] * cotangent.astype(jnp.float32)).astype(jnp.bfloat16)
    positions = jax.vmap(lambda route_block: slot_positions(route_block, N_EXPERT, CAP))(
        routing.reshape(N_SECTION * N_EXPERT, TOK_DEV, 1))

    def place(values, where_to):
        return jnp.zeros((slot_count, D), values.dtype).at[where_to].set(values)

    send_tokens = jax.vmap(place)(tokens.reshape(N_SECTION * N_EXPERT, TOK_DEV, D), positions)
    send_grads = jax.vmap(place)(scaled.reshape(N_SECTION * N_EXPERT, TOK_DEV, D), positions)

    def to_groups(buffer):
        buffer = buffer.reshape(2, groups, N_EXPERT, N_EXPERT, CAP, D)
        buffer = buffer.transpose(1, 3, 0, 2, 4, 5)
        return buffer.reshape(groups, N_EXPERT, 2 * slot_count, D)

    def from_groups(buffer):
        buffer = buffer.reshape(groups, N_EXPERT, 2, N_EXPERT, CAP, D)
        buffer = buffer.transpose(2, 0, 3, 1, 4, 5)
        return buffer.reshape(N_SECTION * N_EXPERT, slot_count, D)

    up_full = up_weight.reshape(2, groups, N_EXPERT, D, half_ff).transpose(1, 2, 3, 0, 4).reshape(groups, N_EXPERT, D, FF)
    down_full = down_weight.reshape(2, groups, N_EXPERT, half_ff, D).transpose(1, 2, 0, 3, 4).reshape(groups, N_EXPERT, FF, D)
    results = lax.map(group_pass, (to_groups(send_tokens), to_groups(send_grads), up_full, down_full))
    output_rows, input_grad, grad_up, grad_down = results

    def pick(buffer, where_to):
        return buffer[where_to]

    picked = jax.vmap(pick)(from_groups(output_rows), positions).reshape(TOKENS, D)
    token_grad = jax.vmap(pick)(from_groups(input_grad), positions).reshape(TOKENS, D)
    mixed = (gate_prob[:, None] * picked.astype(jnp.float32)).astype(jnp.bfloat16)
    grad_up_out = grad_up.reshape(groups, N_EXPERT, D, 2, half_ff).transpose(3, 0, 1, 2, 4).reshape(2 * EXPERTS, D, half_ff)
    grad_down_out = grad_down.reshape(groups, N_EXPERT, 2, half_ff, D).transpose(2, 0, 1, 3, 4).reshape(2 * EXPERTS, half_ff, D)
    return (mixed, token_grad, grad_up_out, grad_down_out)
```

```python
import jax
import jax.numpy as jnp
from jax import lax
from jax.experimental import pallas as pl
from jax.experimental.pallas import tpu as pltpu
from jax.sharding import PartitionSpec as P

F32 = jnp.float32
BF16 = jnp.bfloat16
VMEM_LIMIT = 48 * 1024 * 1024


def exchange(array, axis, flip):
    return lax.ppermute(array, axis, [(i, i ^ flip) for i in range(lax.axis_size(axis))])


def dot(a, b, contract):
    return lax.dot_general(a, b, (contract, ((), ())), preferred_element_type=F32)


def call(body, out_shape, *args):
    return pl.pallas_call(
        body,
        out_shape=out_shape,
        compiler_params=pltpu.CompilerParams(vmem_limit_bytes=VMEM_LIMIT),
    )(*args)


def shape(rows, columns, dtype=BF16):
    return jax.ShapeDtypeStruct((rows, columns), dtype)


def slot_positions(route_row, device, experts, capacity):
    local = route_row.shape[1]

    def body(device_ref, route_ref, slot_ref):
        route = route_ref[...]
        expert = lax.broadcasted_iota(jnp.int32, (experts, local), 0)
        choose = jnp.where(expert == route, 1.0, 0.0)
        earlier = lax.broadcasted_iota(jnp.int32, (local, local), 0)
        later = lax.broadcasted_iota(jnp.int32, (local, local), 1)
        upto = jnp.where(earlier <= later, 1.0, 0.0).astype(BF16)
        running = dot(choose.astype(BF16), upto, ((1,), (0,)))
        rank = jnp.sum(running * choose, axis=0, keepdims=True) - 1.0
        slot_ref[...] = (route ^ device_ref[0]) * capacity + rank.astype(jnp.int32)

    return pl.pallas_call(
        body,
        out_shape=shape(1, local, jnp.int32),
        in_specs=[
            pl.BlockSpec(memory_space=pltpu.SMEM),
            pl.BlockSpec(memory_space=pltpu.VMEM),
        ],
    )(device, route_row)


def dispatch(slots, values, blocks, rows):
    local, width = values.shape

    def body(slot_ref, value_ref, *outs):
        number = lax.broadcasted_iota(jnp.int32, (blocks * rows, local), 0)
        placing = jnp.where(number == slot_ref[...], 1.0, 0.0).astype(BF16)
        placed = dot(placing, value_ref[...], ((1,), (0,))).astype(BF16)
        for block, out in enumerate(outs):
            out[...] = placed[block * rows : (block + 1) * rows]

    return call(body, [shape(rows, width)] * blocks, slots, values)


def collect(slots, parts):
    blocks = len(parts)
    rows, width = parts[0].shape
    local = slots.shape[1]

    def body(slot_ref, *refs):
        out = refs[-1]
        row = lax.broadcasted_iota(jnp.int32, (local, local), 0)
        column = lax.broadcasted_iota(jnp.int32, (local, local), 1)
        wanted = jnp.where(row == column, slot_ref[...].astype(F32), 0.0)
        wanted = jnp.sum(wanted, axis=1, keepdims=True).astype(jnp.int32)
        number = lax.broadcasted_iota(jnp.int32, (local, blocks * rows), 1)
        picking = jnp.where(number == wanted, 1.0, 0.0).astype(BF16)
        every = jnp.concatenate([ref[...] for ref in refs[:-1]], axis=0)
        out[...] = dot(picking, every, ((1,), (0,))).astype(BF16)

    return call(body, shape(local, width), slots, *parts)


def rows_of(refs, which, capacity):
    return jnp.concatenate(
        [ref[which * capacity : (which + 1) * capacity, :] for ref in refs], axis=0
    )


def forward(parts, ups, downs, capacity):
    blocks = len(parts)
    width, half = ups[0].shape
    count = blocks * capacity

    def body(*refs):
        tokens, refs = refs[:blocks], refs[blocks:]
        up, down, refs = refs[:2], refs[2:4], refs[4:]
        outs, hiddens, slopes = refs[:blocks], refs[blocks : blocks + 2], refs[blocks + 2 :]
        for which in range(2):
            preact = dot(rows_of(tokens, which, capacity), up[which][...], ((1,), (0,)))
            square = preact * preact
            tangent = jnp.tanh(0.7978845608 * (preact + 0.044715 * preact * square))
            hidden = (0.5 * preact * (1.0 + tangent)).astype(BF16)
            slope = 0.5 * (1.0 + tangent) + 0.5 * preact * (1.0 - tangent * tangent) * (
                0.7978845608 * (1.0 + 0.134145 * square)
            )
            hiddens[which][...] = hidden
            slopes[which][...] = slope.astype(BF16)
            result = dot(hidden, down[which][...], ((1,), (0,))).astype(BF16)
            for block, out in enumerate(outs):
                out[which * capacity : (which + 1) * capacity, :] = result[
                    block * capacity : (block + 1) * capacity
                ]

    results = call(
        body,
        [shape(2 * capacity, width)] * blocks + [shape(count, half)] * 4,
        *parts,
        *ups,
        *downs,
    )
    return results[:blocks], results[blocks : blocks + 2], results[blocks + 2 :]


def backward(parts, slopes, ups, downs, capacity):
    blocks = len(parts)
    width, half = ups[0].shape
    count = blocks * capacity

    def body(*refs):
        grads, refs = refs[:blocks], refs[blocks:]
        slope, up, down, refs = refs[:2], refs[2:4], refs[4:6], refs[6:]
        outs, hidden_grads = refs[:blocks], refs[blocks:]
        for which in range(2):
            through = dot(rows_of(grads, which, capacity), down[which][...], ((1,), (1,)))
            hidden_grad = (through * slope[which][...].astype(F32)).astype(BF16)
            hidden_grads[which][...] = hidden_grad
            result = dot(hidden_grad, up[which][...], ((1,), (1,))).astype(BF16)
            for block, out in enumerate(outs):
                out[which * capacity : (which + 1) * capacity, :] = result[
                    block * capacity : (block + 1) * capacity
                ]

    results = call(
        body,
        [shape(2 * capacity, width)] * blocks + [shape(count, half)] * 2,
        *parts,
        *slopes,
        *ups,
        *downs,
    )
    return results[:blocks], results[blocks:]


def weight_gradients(which, token_parts, grad_parts, hiddens, hidden_grads, capacity, dtype):
    blocks = len(token_parts)
    width = token_parts[0].shape[1]
    half = hiddens[0].shape[1]

    def body(*refs):
        tokens, refs = refs[:blocks], refs[blocks:]
        grads, refs = refs[:blocks], refs[blocks:]
        hidden, hidden_grad, refs = refs[:2], refs[2:4], refs[4:]
        up_out, down_out = refs
        rows = rows_of(tokens, which, capacity)
        both = jnp.concatenate([ref[...] for ref in hidden_grad], axis=0)
        up_out[...] = dot(rows, both, ((0,), (0,))).astype(dtype)
        rows = rows_of(grads, which, capacity)
        both = jnp.concatenate([ref[...] for ref in hidden], axis=0)
        down_out[...] = dot(both, rows, ((0,), (0,))).astype(dtype)

    return call(
        body,
        [shape(width, half, dtype), shape(half, width, dtype)],
        *token_parts,
        *grad_parts,
        *hiddens,
        *hidden_grads,
    )


def spread(parts):
    return [parts[0]] + [exchange(part, "expert", 2 * m) for m, part in enumerate(parts) if m]


def shards(tokens, gate_prob, routing, up_weight, down_weight, cotangent):
    experts = lax.axis_size("expert")
    opposite = lax.axis_size("section") // 2
    local = tokens.shape[0]
    capacity = -(-2 * local // experts // 16) * 16
    blocks = experts // 2
    device = lax.axis_index("expert").astype(jnp.int32).reshape(1)

    def across(array):
        return exchange(array, "section", opposite)

    pair_tokens = across(tokens)
    slots = slot_positions(routing.reshape(1, local), device, experts, capacity)
    pair_slots = across(slots)
    ups = (up_weight[0], exchange(up_weight[0], "expert", 1))
    downs = (down_weight[0], exchange(down_weight[0], "expert", 1))
    scaled = (gate_prob[:, None] * cotangent.astype(F32)).astype(BF16)
    own_x = spread(dispatch(slots, tokens, blocks, 2 * capacity))
    own_c = spread(dispatch(slots, scaled, blocks, 2 * capacity))
    later_scaled, _ = lax.optimization_barrier((scaled, pair_tokens))
    pair_scaled = across(later_scaled)

    pair_x = spread(dispatch(pair_slots, pair_tokens, blocks, 2 * capacity))
    pair_out, pair_hidden, pair_slope = forward(pair_x, ups, downs, capacity)
    pair_out = across(collect(pair_slots, spread(pair_out)))
    own_out, own_hidden, own_slope = forward(own_x, ups, downs, capacity)
    own_out = collect(slots, spread(own_out))

    pair_c = spread(dispatch(pair_slots, pair_scaled, blocks, 2 * capacity))
    pair_back, pair_hidden_grad = backward(pair_c, pair_slope, ups, downs, capacity)
    pair_back = across(collect(pair_slots, spread(pair_back)))
    own_back, own_hidden_grad = backward(own_c, own_slope, ups, downs, capacity)
    own_back = collect(slots, spread(own_back))

    def gradients(which, dtype):
        return weight_gradients(
            which,
            own_x + pair_x,
            own_c + pair_c,
            (own_hidden[which], pair_hidden[which]),
            (own_hidden_grad[which], pair_hidden_grad[which]),
            capacity,
            dtype,
        )

    give_up, give_down = gradients(1, BF16)
    peer_up, peer_down = exchange(give_up, "expert", 1), exchange(give_down, "expert", 1)
    keep_up, keep_down = gradients(0, F32)
    grad_up = (keep_up + peer_up.astype(F32)).astype(BF16)
    grad_down = (keep_down + peer_down.astype(F32)).astype(BF16)
    out = (own_out.astype(F32) + pair_out.astype(F32)).astype(BF16)
    mixed = (gate_prob[:, None] * out.astype(F32)).astype(BF16)
    token_grad = (own_back.astype(F32) + pair_back.astype(F32)).astype(BF16)
    return (mixed, token_grad, grad_up[None], grad_down[None])


def solution(mesh):
    in_specs = (
        P(("section", "expert"), None),
        P(("section", "expert")),
        P(("section", "expert"), None),
        P(("section", "expert"), None, None),
        P(("section", "expert"), None, None),
        P(("section", "expert"), None),
    )
    out_specs = (
        P(("section", "expert"), None),
        P(("section", "expert"), None),
        P(("section", "expert"), None, None),
        P(("section", "expert"), None, None),
    )
    return jax.shard_map(shards, mesh=mesh, in_specs=in_specs, out_specs=out_specs, check_vma=False)
```

```python
import math

import jax
import jax.numpy as jnp
from jax import lax
from jax.experimental import pallas as pl
from jax.experimental.pallas import tpu as pltpu
from jax.sharding import PartitionSpec as P

F32 = jnp.float32
BF16 = jnp.bfloat16
VMEM_LIMIT = 48 * 1024 * 1024


def exchange(array, axis, flip):
    return lax.ppermute(array, axis, [(i, i ^ flip) for i in range(lax.axis_size(axis))])


def dot(a, b, contract):
    return lax.dot_general(a, b, (contract, ((), ())), preferred_element_type=F32)


def call(body, out_shape, *args, after=()):
    waits = len(after)

    def kernel(*refs):
        body(*refs[waits:])

    return pl.pallas_call(
        kernel,
        out_shape=out_shape,
        in_specs=[pl.BlockSpec(memory_space=pl.ANY)] * waits
        + [pl.BlockSpec(memory_space=pltpu.VMEM)] * len(args),
        cost_estimate=pl.CostEstimate(flops=1, bytes_accessed=1, transcendentals=0),
        compiler_params=pltpu.CompilerParams(vmem_limit_bytes=VMEM_LIMIT),
    )(*after, *args)


def column(row):
    count = row.shape[1]
    down = lax.broadcasted_iota(jnp.int32, (count, count), 0)
    along = lax.broadcasted_iota(jnp.int32, (count, count), 1)
    return jnp.sum(jnp.where(down == along, row, 0.0), axis=1, keepdims=True)


def shape(rows, columns, dtype=BF16):
    return jax.ShapeDtypeStruct((rows, columns), dtype)


def slot_positions(route_row, device, experts, capacity):
    local = route_row.shape[1]

    def body(device_ref, route_ref, slot_ref):
        route = route_ref[...]
        expert = lax.broadcasted_iota(jnp.int32, (experts, local), 0)
        choose = jnp.where(expert == route, 1.0, 0.0)
        earlier = lax.broadcasted_iota(jnp.int32, (local, local), 0)
        later = lax.broadcasted_iota(jnp.int32, (local, local), 1)
        upto = jnp.where(earlier <= later, 1.0, 0.0).astype(BF16)
        running = dot(choose.astype(BF16), upto, ((1,), (0,)))
        rank = jnp.sum(running * choose, axis=0, keepdims=True) - 1.0
        slot_ref[...] = (route ^ device_ref[0]) * capacity + rank.astype(jnp.int32)

    return pl.pallas_call(
        body,
        out_shape=shape(1, local, jnp.int32),
        in_specs=[
            pl.BlockSpec(memory_space=pltpu.SMEM),
            pl.BlockSpec(memory_space=pltpu.VMEM),
        ],
    )(device, route_row)


def dispatch(slots, tokens, scaling, blocks, rows, mode, after=()):
    local, width = tokens.shape
    placed_arrays = 2 if mode == "place" else 1

    def body(slot_ref, token_ref, *refs):
        outs = refs[len(scaling) :]
        values = [token_ref[...]]
        if scaling:
            scaled = column(refs[0][...]) * refs[1][...].astype(F32)
            values.append(scaled.astype(BF16))
        number = lax.broadcasted_iota(jnp.int32, (blocks * rows, local), 0)
        placing = jnp.where(number == slot_ref[...], 1.0, 0.0).astype(BF16)
        for which in range(placed_arrays):
            placed = dot(placing, values[which], ((1,), (0,))).astype(BF16)
            for block in range(blocks):
                outs[block][which * rows : (which + 1) * rows, :] = placed[
                    block * rows : (block + 1) * rows
                ]
        if mode == "give":
            outs[blocks][...] = values[1]

    shapes = [shape(placed_arrays * rows, width)] * blocks + [shape(local, width)] * (mode == "give")
    return call(body, shapes, slots, tokens, *scaling, after=after)


def picked(slot_row, refs, base, rows):
    wanted = column(slot_row.astype(F32)).astype(jnp.int32)
    number = lax.broadcasted_iota(jnp.int32, (slot_row.shape[1], len(refs) * rows), 1)
    picking = jnp.where(number == wanted, 1.0, 0.0).astype(BF16)
    every = jnp.concatenate([ref[base : base + rows, :] for ref in refs], axis=0)
    return dot(picking, every, ((1,), (0,)))


def collect(slots, parts, after=()):
    blocks = len(parts)
    rows, width = parts[0].shape

    def body(slot_ref, *refs):
        refs[-1][...] = picked(slot_ref[...], refs[:blocks], 0, rows).astype(BF16)

    return call(body, shape(slots.shape[1], width), slots, *parts, after=after)


def collect_own(slots, parts, other_out, gate, after=()):
    blocks = len(parts)
    rows, width = parts[0].shape[0] // 2, parts[0].shape[1]
    local = slots.shape[1]

    def body(slot_ref, *refs):
        parts, (other_ref, gate_ref, mixed_ref, back_ref) = refs[:blocks], refs[blocks:]
        out = picked(slot_ref[...], parts, 0, rows) + other_ref[...].astype(F32)
        mixed_ref[...] = (column(gate_ref[...]) * out.astype(BF16).astype(F32)).astype(BF16)
        back_ref[...] = picked(slot_ref[...], parts, rows, rows).astype(BF16)

    return call(body, [shape(local, width)] * 2, slots, *parts, other_out, gate, after=after)


def rows_of(refs, which, capacity, base=0):
    start = base + which * capacity
    return jnp.concatenate([ref[start : start + capacity, :] for ref in refs], axis=0)


def put_rows(refs, which, capacity, base, result):
    start = base + which * capacity
    for block, ref in enumerate(refs):
        ref[start : start + capacity, :] = result[block * capacity : (block + 1) * capacity]


def activation(preact):
    square = preact * preact
    tangent = jnp.tanh(0.7978845608 * (preact + 0.044715 * preact * square))
    hidden = 0.5 * preact * (1.0 + tangent)
    slope = 0.5 * (1.0 + tangent) + 0.5 * preact * (1.0 - tangent * tangent) * (
        0.7978845608 * (1.0 + 0.134145 * square)
    )
    return hidden.astype(BF16), slope


def forward(parts, ups, downs, capacity, after=()):
    blocks = len(parts)
    width, half = ups[0].shape
    count = blocks * capacity

    def body(*refs):
        tokens, refs = refs[:blocks], refs[blocks:]
        up, down, refs = refs[:2], refs[2:4], refs[4:]
        outs, hiddens, slopes = refs[:blocks], refs[blocks : blocks + 2], refs[blocks + 2 :]
        for which in range(2):
            preact = dot(rows_of(tokens, which, capacity), up[which][...], ((1,), (0,)))
            hidden, slope = activation(preact)
            hiddens[which][...] = hidden
            slopes[which][...] = slope.astype(BF16)
            result = dot(hidden, down[which][...], ((1,), (0,))).astype(BF16)
            put_rows(outs, which, capacity, 0, result)

    shapes = [shape(2 * capacity, width)] * blocks + [shape(count, half)] * 4
    results = call(body, shapes, *parts, *ups, *downs, after=after)
    return results[:blocks], results[blocks : blocks + 2], results[blocks + 2 :]


def backward(parts, slopes, ups, downs, capacity, after=()):
    blocks = len(parts)
    width, half = ups[0].shape
    count = blocks * capacity

    def body(*refs):
        grads, refs = refs[:blocks], refs[blocks:]
        slope, up, down, refs = refs[:2], refs[2:4], refs[4:6], refs[6:]
        outs, hidden_grads = refs[:blocks], refs[blocks:]
        for which in range(2):
            through = dot(rows_of(grads, which, capacity), down[which][...], ((1,), (1,)))
            hidden_grad = (through * slope[which][...].astype(F32)).astype(BF16)
            hidden_grads[which][...] = hidden_grad
            result = dot(hidden_grad, up[which][...], ((1,), (1,))).astype(BF16)
            put_rows(outs, which, capacity, 0, result)

    shapes = [shape(2 * capacity, width)] * blocks + [shape(count, half)] * 2
    results = call(body, shapes, *parts, *slopes, *ups, *downs, after=after)
    return results[:blocks], results[blocks:]


def both_ways(parts, ups, downs, capacity, after=()):
    blocks = len(parts)
    width, half = ups[0].shape
    count = blocks * capacity
    base = 2 * capacity

    def body(*refs):
        parts, refs = refs[:blocks], refs[blocks:]
        up, down, refs = refs[:2], refs[2:4], refs[4:]
        outs, hiddens, hidden_grads = refs[:blocks], refs[blocks : blocks + 2], refs[blocks + 2 :]
        for which in range(2):
            preact = dot(rows_of(parts, which, capacity), up[which][...], ((1,), (0,)))
            hidden, slope = activation(preact)
            hiddens[which][...] = hidden
            result = dot(hidden, down[which][...], ((1,), (0,))).astype(BF16)
            put_rows(outs, which, capacity, 0, result)
            through = dot(rows_of(parts, which, capacity, base), down[which][...], ((1,), (1,)))
            hidden_grad = (through * slope).astype(BF16)
            hidden_grads[which][...] = hidden_grad
            result = dot(hidden_grad, up[which][...], ((1,), (1,))).astype(BF16)
            put_rows(outs, which, capacity, base, result)

    shapes = [shape(2 * base, width)] * blocks + [shape(count, half)] * 4
    results = call(body, shapes, *parts, *ups, *downs, after=after)
    return results[:blocks], results[blocks : blocks + 2], results[blocks + 2 :]


def panels(array, size):
    return [array[:, start : start + size] for start in range(0, array.shape[1], size)]


def weight_gradients(which, own, pair_x, pair_c, hiddens, hidden_grads, capacity, peer=None, after=()):
    blocks = len(pair_x)
    width = pair_x[0].shape[1]
    half = hiddens[0].shape[1]
    size = math.gcd(width, half)
    more = () if peer is None else (peer,)

    def body(*refs):
        own, refs = refs[:blocks], refs[blocks:]
        tokens, grads, refs = refs[:blocks], refs[blocks : 2 * blocks], refs[2 * blocks :]
        hidden, hidden_grad, refs = refs[:2], refs[2:4], refs[4:]
        both = [jnp.concatenate([ref[...] for ref in pair], axis=0) for pair in (hidden, hidden_grad)]
        rows = [rows_of(own, which, capacity), rows_of(tokens, which, capacity)]
        up = dot(jnp.concatenate(rows, axis=0), both[1], ((0,), (0,)))
        rows = [rows_of(own, which, capacity, 2 * capacity), rows_of(grads, which, capacity)]
        down = dot(both[0], jnp.concatenate(rows, axis=0), ((0,), (0,)))
        start = 0
        for number, result in enumerate((up, down)):
            for place, panel in enumerate(panels(result, size)):
                stop = start + panel.shape[0]
                if peer is None:
                    refs[0][start:stop, :] = panel.astype(BF16)
                else:
                    total = panel + refs[0][start:stop, :].astype(F32)
                    refs[1 + number][:, place * size : (place + 1) * size] = total.astype(BF16)
                start = stop

    if peer is None:
        shapes = shape(2 * width * half // size, size)
    else:
        shapes = [shape(width, half), shape(half, width)]
    return call(body, shapes, *own, *pair_x, *pair_c, *hiddens, *hidden_grads, *more, after=after)


def added(one, other, after=()):
    def body(one_ref, other_ref, out):
        out[...] = (one_ref[...].astype(F32) + other_ref[...].astype(F32)).astype(BF16)

    return call(body, shape(*one.shape), one, other, after=after)


def spread(parts):
    return [parts[0]] + [exchange(part, "expert", 2 * m) for m, part in enumerate(parts) if m]


def shards(tokens, gate_prob, routing, up_weight, down_weight, cotangent):
    experts = lax.axis_size("expert")
    opposite = lax.axis_size("section") // 2
    local = tokens.shape[0]
    capacity = -(-2 * local // experts // 16) * 16
    blocks = experts // 2
    device = lax.axis_index("expert").astype(jnp.int32).reshape(1)

    def across(array):
        return exchange(array, "section", opposite)

    rows = 2 * capacity
    gate = gate_prob.reshape(1, local)
    pair_tokens = across(tokens)
    slots = slot_positions(routing.reshape(1, local), device, experts, capacity)
    pair_slots = across(slots)
    ups = (up_weight[0], exchange(up_weight[0], "expert", 1))
    downs = (down_weight[0], exchange(down_weight[0], "expert", 1))

    scaling = (gate, cotangent)
    sent = dispatch(slots, tokens, scaling, blocks, rows, "place", after=(ups[1], downs[1]))
    own = spread(sent)
    *sent, scaled = dispatch(
        pair_slots, pair_tokens, scaling, blocks, rows, "give", after=(sent[0],)
    )
    pair_x = spread(sent)
    pair_scaled = across(scaled)
    own_sent, own_hidden, own_hidden_grad = both_ways(
        own, ups, downs, capacity, after=(sent[0],)
    )
    sent, pair_hidden, pair_slope = forward(pair_x, ups, downs, capacity, after=(own_sent[0],))
    back = spread(sent)
    sent = dispatch(pair_slots, pair_scaled, (), blocks, rows, "", after=(sent[0],))
    pair_c = spread(sent)
    term = collect(pair_slots, back, after=(sent[0],))
    other_out = across(term)
    sent, pair_hidden_grad = backward(pair_c, pair_slope, ups, downs, capacity, after=(term,))
    back = spread(sent)

    def gradients(which, peer, after):
        return weight_gradients(
            which,
            own,
            pair_x,
            pair_c,
            (own_hidden[which], pair_hidden[which]),
            (own_hidden_grad[which], pair_hidden_grad[which]),
            capacity,
            peer,
            after,
        )

    term = collect(pair_slots, back, after=(other_out,))
    other_back = across(term)
    give = gradients(1, None, (term,))
    peer = exchange(give, "expert", 1)
    own_back = spread(own_sent)
    grad_up, grad_down = gradients(0, peer, ())
    mixed, own_term = collect_own(slots, own_back, other_out, gate, after=(grad_up,))
    token_grad = added(own_term, other_back, after=(mixed,))
    return (mixed, token_grad, grad_up[None], grad_down[None])


def solution(mesh):
    in_specs = (
        P(("section", "expert"), None),
        P(("section", "expert")),
        P(("section", "expert"), None),
        P(("section", "expert"), None, None),
        P(("section", "expert"), None, None),
        P(("section", "expert"), None),
    )
    out_specs = (
        P(("section", "expert"), None),
        P(("section", "expert"), None),
        P(("section", "expert"), None, None),
        P(("section", "expert"), None, None),
    )
    return jax.shard_map(shards, mesh=mesh, in_specs=in_specs, out_specs=out_specs, check_vma=False)
```

```python
import math

import jax
import jax.numpy as jnp
from jax import lax
from jax.experimental import pallas as pl
from jax.experimental.pallas import tpu as pltpu
from jax.sharding import PartitionSpec as P

F32 = jnp.float32
BF16 = jnp.bfloat16
VMEM_LIMIT = 48 * 1024 * 1024


def exchange(array, axis, flip):
    return lax.ppermute(array, axis, [(i, i ^ flip) for i in range(lax.axis_size(axis))])


def dot(a, b, contract):
    return lax.dot_general(a, b, (contract, ((), ())), preferred_element_type=F32)


def call(body, out_shape, *args, after=(), space=pl.ANY, flops=1):
    waits = len(after)

    def kernel(*refs):
        body(*refs[waits:])

    return pl.pallas_call(
        kernel,
        out_shape=out_shape,
        in_specs=[pl.BlockSpec(memory_space=space)] * waits
        + [pl.BlockSpec(memory_space=pltpu.VMEM)] * len(args),
        cost_estimate=pl.CostEstimate(flops=flops, bytes_accessed=1, transcendentals=0),
        compiler_params=pltpu.CompilerParams(vmem_limit_bytes=VMEM_LIMIT),
    )(*after, *args)


def column(row):
    count = row.shape[1]
    down = lax.broadcasted_iota(jnp.int32, (count, count), 0)
    along = lax.broadcasted_iota(jnp.int32, (count, count), 1)
    return jnp.sum(jnp.where(down == along, row, 0.0), axis=1, keepdims=True)


def shape(rows, columns, dtype=BF16):
    return jax.ShapeDtypeStruct((rows, columns), dtype)


def prepare(device, route_row, gate, tokens, cotangent, blocks, capacity):
    local, width = tokens.shape
    experts = 2 * blocks
    pieces = 4
    piece = local // pieces

    def body(device_ref, route_ref, gate_ref, token_ref, cotangent_ref, slot_ref, *refs):
        token_out, scaled_out, cotangent_here, sems = refs
        copies = [
            pltpu.make_async_copy(
                source.at[number * piece : (number + 1) * piece],
                target.at[number * piece : (number + 1) * piece],
                sems.at[array * pieces + number],
            )
            for array, (source, target) in enumerate(
                ((token_ref, token_out), (cotangent_ref, cotangent_here))
            )
            for number in range(pieces)
        ]
        for copy in copies:
            copy.start()
        route = route_ref[...]
        expert = lax.broadcasted_iota(jnp.int32, (experts, local), 0)
        choose = jnp.where(expert == route, 1.0, 0.0)
        earlier = lax.broadcasted_iota(jnp.int32, (local, local), 0)
        later = lax.broadcasted_iota(jnp.int32, (local, local), 1)
        upto = jnp.where(earlier <= later, 1.0, 0.0).astype(BF16)
        running = dot(choose.astype(BF16), upto, ((1,), (0,)))
        rank = jnp.sum(running * choose, axis=0, keepdims=True) - 1.0
        slot_ref[...] = (route ^ device_ref[0]) * capacity + rank.astype(jnp.int32)
        factor = column(gate_ref[...].reshape(1, local))
        for copy in copies:
            copy.wait()
        scaled_out[...] = (factor * cotangent_here[...].astype(F32)).astype(BF16)

    return pl.pallas_call(
        body,
        out_shape=[shape(1, local, jnp.int32), shape(local, width), shape(local, width)],
        in_specs=[pl.BlockSpec(memory_space=pltpu.SMEM)]
        + [pl.BlockSpec(memory_space=pltpu.VMEM)] * 2
        + [pl.BlockSpec(memory_space=pltpu.HBM)] * 2,
        out_specs=[pl.BlockSpec(memory_space=pltpu.VMEM)] * 3,
        scratch_shapes=[
            pltpu.VMEM((local, width), BF16),
            pltpu.SemaphoreType.DMA((2 * pieces,)),
        ],
        cost_estimate=pl.CostEstimate(flops=1, bytes_accessed=1, transcendentals=0),
        compiler_params=pltpu.CompilerParams(vmem_limit_bytes=VMEM_LIMIT),
    )(
        device,
        route_row,
        gate,
        pltpu.with_memory_space_constraint(tokens, pltpu.HBM),
        pltpu.with_memory_space_constraint(cotangent, pltpu.HBM),
    )


def dispatch(slots, arrays, blocks, rows, given=None, after=()):
    local, width = arrays[0].shape
    several = len(arrays)
    more = () if given is None else (given,)

    def body(slot_ref, *refs):
        values, outs = refs[:several], refs[several + len(more) :]
        number = lax.broadcasted_iota(jnp.int32, (blocks * rows, local), 0)
        placing = jnp.where(number == slot_ref[...], 1.0, 0.0).astype(BF16)
        for which in range(several):
            placed = dot(placing, values[which][...], ((1,), (0,))).astype(BF16)
            for block in range(blocks):
                outs[block][which * rows : (which + 1) * rows, :] = placed[
                    block * rows : (block + 1) * rows
                ]
        if more:
            outs[blocks][...] = refs[several][...]

    shapes = [shape(several * rows, width)] * blocks + [shape(local, width)] * len(more)
    return call(body, shapes, slots, *arrays, *more, after=after)


def picked(slot_row, refs, base, rows):
    wanted = column(slot_row.astype(F32)).astype(jnp.int32)
    number = lax.broadcasted_iota(jnp.int32, (slot_row.shape[1], len(refs) * rows), 1)
    picking = jnp.where(number == wanted, 1.0, 0.0).astype(BF16)
    every = jnp.concatenate([ref[base : base + rows, :] for ref in refs], axis=0)
    return dot(picking, every, ((1,), (0,)))


def collect(slots, parts, after=()):
    blocks = len(parts)
    rows, width = parts[0].shape

    def body(slot_ref, *refs):
        refs[blocks][...] = picked(slot_ref[...], refs[:blocks], 0, rows).astype(BF16)

    return call(body, shape(slots.shape[1], width), slots, *parts, after=after)


def collect_own(slots, parts, other_out, gate, after=()):
    blocks = len(parts)
    rows, width = parts[0].shape[0] // 2, parts[0].shape[1]
    local = slots.shape[1]

    def body(slot_ref, *refs):
        parts, (other_ref, gate_ref, mixed_ref, back_ref) = refs[:blocks], refs[blocks:]
        out = picked(slot_ref[...], parts, 0, rows) + other_ref[...].astype(F32)
        mixed_ref[...] = (column(gate_ref[...].reshape(1, local)) * out.astype(BF16).astype(F32)).astype(BF16)
        back_ref[...] = picked(slot_ref[...], parts, rows, rows).astype(BF16)

    return call(
        body,
        [shape(local, width)] * 2,
        slots,
        *parts,
        other_out,
        gate,
        after=after,
        space=pltpu.HBM,
    )


def rows_of(refs, which, capacity, base=0):
    start = base + which * capacity
    return jnp.concatenate([ref[start : start + capacity, :] for ref in refs], axis=0)


def put_rows(refs, which, capacity, base, result):
    start = base + which * capacity
    for block, ref in enumerate(refs):
        ref[start : start + capacity, :] = result[block * capacity : (block + 1) * capacity]


def activation(preact):
    square = preact * preact
    tangent = jnp.tanh(0.7978845608 * (preact + 0.044715 * preact * square))
    hidden = 0.5 * preact * (1.0 + tangent)
    slope = 0.5 * (1.0 + tangent) + 0.5 * preact * (1.0 - tangent * tangent) * (
        0.7978845608 * (1.0 + 0.134145 * square)
    )
    return hidden.astype(BF16), slope


def forward(parts, ups, downs, capacity, after=()):
    blocks = len(parts)
    width, half = ups[0].shape
    count = blocks * capacity

    def body(*refs):
        tokens, refs = refs[:blocks], refs[blocks:]
        up, down, refs = refs[:2], refs[2:4], refs[4:]
        outs, hiddens, slopes = refs[:blocks], refs[blocks : blocks + 2], refs[blocks + 2 :]
        for which in range(2):
            preact = dot(rows_of(tokens, which, capacity), up[which][...], ((1,), (0,)))
            hidden, slope = activation(preact)
            hiddens[which][...] = hidden
            slopes[which][...] = slope.astype(BF16)
            result = dot(hidden, down[which][...], ((1,), (0,))).astype(BF16)
            put_rows(outs, which, capacity, 0, result)

    shapes = [shape(2 * capacity, width)] * blocks + [shape(count, half)] * 4
    results = call(body, shapes, *parts, *ups, *downs, after=after)
    return results[:blocks], results[blocks : blocks + 2], results[blocks + 2 :]


def backward(parts, slopes, ups, downs, capacity, after=()):
    blocks = len(parts)
    width, half = ups[0].shape
    count = blocks * capacity

    def body(*refs):
        grads, refs = refs[:blocks], refs[blocks:]
        slope, up, down, refs = refs[:2], refs[2:4], refs[4:6], refs[6:]
        outs, hidden_grads = refs[:blocks], refs[blocks:]
        for which in range(2):
            through = dot(rows_of(grads, which, capacity), down[which][...], ((1,), (1,)))
            hidden_grad = (through * slope[which][...].astype(F32)).astype(BF16)
            hidden_grads[which][...] = hidden_grad
            result = dot(hidden_grad, up[which][...], ((1,), (1,))).astype(BF16)
            put_rows(outs, which, capacity, 0, result)

    shapes = [shape(2 * capacity, width)] * blocks + [shape(count, half)] * 2
    results = call(body, shapes, *parts, *slopes, *ups, *downs, after=after)
    return results[:blocks], results[blocks:]


def both_ways(parts, ups, downs, capacity, after=()):
    blocks = len(parts)
    width, half = ups[0].shape
    count = blocks * capacity
    base = 2 * capacity

    def body(*refs):
        parts, refs = refs[:blocks], refs[blocks:]
        up, down, refs = refs[:2], refs[2:4], refs[4:]
        outs, hiddens, hidden_grads = refs[:blocks], refs[blocks : blocks + 2], refs[blocks + 2 :]
        for which in range(2):
            preact = dot(rows_of(parts, which, capacity), up[which][...], ((1,), (0,)))
            hidden, slope = activation(preact)
            hiddens[which][...] = hidden
            result = dot(hidden, down[which][...], ((1,), (0,))).astype(BF16)
            put_rows(outs, which, capacity, 0, result)
            through = dot(rows_of(parts, which, capacity, base), down[which][...], ((1,), (1,)))
            hidden_grad = (through * slope).astype(BF16)
            hidden_grads[which][...] = hidden_grad
            result = dot(hidden_grad, up[which][...], ((1,), (1,))).astype(BF16)
            put_rows(outs, which, capacity, base, result)

    shapes = [shape(2 * base, width)] * blocks + [shape(count, half)] * 4
    results = call(body, shapes, *parts, *ups, *downs, after=after)
    return results[:blocks], results[blocks : blocks + 2], results[blocks + 2 :]


def panels(array, size):
    return [array[:, start : start + size] for start in range(0, array.shape[1], size)]


def weight_gradients(which, own, pair_x, pair_c, hiddens, hidden_grads, capacity, dtype, after=(), flops=1):
    blocks = len(pair_x)
    width = pair_x[0].shape[1]
    half = hiddens[0].shape[1]
    size = math.gcd(width, half)

    def body(*refs):
        own, refs = refs[:blocks], refs[blocks:]
        tokens, grads, refs = refs[:blocks], refs[blocks : 2 * blocks], refs[2 * blocks :]
        hidden, hidden_grad, out = refs[:2], refs[2:4], refs[4]
        both = [jnp.concatenate([ref[...] for ref in pair], axis=0) for pair in (hidden, hidden_grad)]
        rows = [rows_of(own, which, capacity), rows_of(tokens, which, capacity)]
        up = dot(jnp.concatenate(rows, axis=0), both[1], ((0,), (0,)))
        rows = [rows_of(own, which, capacity, 2 * capacity), rows_of(grads, which, capacity)]
        down = dot(both[0], jnp.concatenate(rows, axis=0), ((0,), (0,)))
        start = 0
        for result in (up, down):
            for panel in panels(result, size):
                out[start : start + panel.shape[0], :] = panel.astype(dtype)
                start += panel.shape[0]

    shapes = shape(2 * width * half // size, size, dtype)
    return call(body, shapes, *own, *pair_x, *pair_c, *hiddens, *hidden_grads, after=after, flops=flops)


def joined(terms, peer, width, half, after=()):
    size = terms.shape[1]

    def body(term_ref, peer_ref, up_ref, down_ref):
        start = 0
        for out in (up_ref, down_ref):
            for place in range(out.shape[1] // size):
                stop = start + out.shape[0]
                total = term_ref[start:stop, :] + peer_ref[start:stop, :].astype(F32)
                out[:, place * size : (place + 1) * size] = total.astype(BF16)
                start = stop

    return call(body, [shape(width, half), shape(half, width)], terms, peer, after=after)


def spread(parts):
    return [parts[0]] + [exchange(part, "expert", 2 * m) for m, part in enumerate(parts) if m]


def shards(tokens, gate_prob, routing, up_weight, down_weight, cotangent):
    experts = lax.axis_size("expert")
    opposite = lax.axis_size("section") // 2
    local = tokens.shape[0]
    capacity = -(-2 * local // experts // 16) * 16
    blocks = experts // 2
    device = lax.axis_index("expert").astype(jnp.int32).reshape(1)

    def across(array):
        return exchange(array, "section", opposite)

    rows = 2 * capacity
    pair_tokens = across(tokens)
    ups = (up_weight[0], exchange(up_weight[0], "expert", 1))
    downs = (down_weight[0], exchange(down_weight[0], "expert", 1))

    slots, tokens, scaled = prepare(
        device, routing.reshape(1, local), gate_prob, tokens, cotangent, blocks, capacity
    )
    sent = dispatch(slots, (tokens, scaled), blocks, rows, after=(ups[1], downs[1]))
    own = spread(sent)
    pair_slots = across(slots)
    *sent, scaled = dispatch(pair_slots, (pair_tokens,), blocks, rows, scaled, after=(sent[0],))
    pair_x = spread(sent)
    pair_scaled = across(scaled)
    own_sent, own_hidden, own_hidden_grad = both_ways(
        own, ups, downs, capacity, after=(sent[0],)
    )
    sent, pair_hidden, pair_slope = forward(pair_x, ups, downs, capacity, after=(own_sent[0],))
    back = spread(sent)
    sent = dispatch(pair_slots, (pair_scaled,), blocks, rows, after=(sent[0],))
    pair_c = spread(sent)
    term = collect(pair_slots, back, after=(sent[0],))
    other_out = across(term)
    sent, pair_hidden_grad = backward(pair_c, pair_slope, ups, downs, capacity, after=(term,))
    back = spread(sent)

    def gradients(which, dtype, after, flops):
        return weight_gradients(
            which,
            own,
            pair_x,
            pair_c,
            (own_hidden[which], pair_hidden[which]),
            (own_hidden_grad[which], pair_hidden_grad[which]),
            capacity,
            dtype,
            after,
            flops,
        )

    term = collect(pair_slots, back, after=(other_out,))
    other_back = across(term)
    own_back = spread(own_sent)
    give = gradients(1, BF16, (term,), 1 * 10**9)
    keep = gradients(0, F32, (give,), 30 * 10**9)
    peer = exchange(give, "expert", 1)
    grad_up, grad_down = joined(keep, peer, *ups[0].shape)
    mixed, own_term = collect_own(slots, own_back, other_out, gate_prob, after=(pltpu.with_memory_space_constraint(grad_up, pltpu.HBM),))
    token_grad = (own_term.astype(F32) + other_back.astype(F32)).astype(BF16)
    return (mixed, token_grad, grad_up[None], grad_down[None])


def solution(mesh):
    in_specs = (
        P(("section", "expert"), None),
        P(("section", "expert")),
        P(("section", "expert"), None),
        P(("section", "expert"), None, None),
        P(("section", "expert"), None, None),
        P(("section", "expert"), None),
    )
    out_specs = (
        P(("section", "expert"), None),
        P(("section", "expert"), None),
        P(("section", "expert"), None, None),
        P(("section", "expert"), None, None),
    )
    return jax.shard_map(shards, mesh=mesh, in_specs=in_specs, out_specs=out_specs, check_vma=False)
```

```python
import math

import jax
import jax.numpy as jnp
from jax import lax
from jax.experimental import pallas as pl
from jax.experimental.pallas import tpu as pltpu
from jax.sharding import PartitionSpec as P

F32 = jnp.float32
BF16 = jnp.bfloat16
VMEM_LIMIT = 48 * 1024 * 1024
HEAVY = pl.CostEstimate(flops=30 * 10**9, bytes_accessed=1, transcendentals=0)
LIGHT = pl.CostEstimate(flops=1, bytes_accessed=1, transcendentals=0)


def exchange(array, axis, flip):
    return lax.ppermute(array, axis, [(i, i ^ flip) for i in range(lax.axis_size(axis))])


def dot(a, b, contract):
    return lax.dot_general(a, b, (contract, ((), ())), preferred_element_type=F32)


def call(body, out_shape, *args, after=(), space=pl.ANY, weight=HEAVY):
    waits = len(after)

    def kernel(*refs):
        body(*refs[waits:])

    return pl.pallas_call(
        kernel,
        out_shape=out_shape,
        in_specs=[pl.BlockSpec(memory_space=space)] * waits
        + [pl.BlockSpec(memory_space=pltpu.VMEM)] * len(args),
        cost_estimate=weight,
        compiler_params=pltpu.CompilerParams(vmem_limit_bytes=VMEM_LIMIT),
    )(*after, *args)


def column(row):
    count = row.shape[1]
    down = lax.broadcasted_iota(jnp.int32, (count, count), 0)
    along = lax.broadcasted_iota(jnp.int32, (count, count), 1)
    return jnp.sum(jnp.where(down == along, row, 0.0), axis=1, keepdims=True)


def shape(rows, columns, dtype=BF16):
    return jax.ShapeDtypeStruct((rows, columns), dtype)


def prepare(device, route_row, gate, tokens, cotangent, blocks, capacity):
    local, width = tokens.shape
    experts = 2 * blocks
    pieces = 4
    piece = local // pieces
    parts = [pl.ds(number * piece, piece) for number in range(pieces)]

    def body(device_ref, route_ref, gate_ref, token_ref, cotangent_ref, *refs):
        slot_ref, token_out, scaled_out, route_here, gate_here, cotangent_here, sems = refs
        pairs = [(route_ref, route_here), (gate_ref, gate_here)]
        pairs += [(cotangent_ref.at[part], cotangent_here.at[part]) for part in parts]
        pairs += [(token_ref.at[part], token_out.at[part]) for part in parts]
        copies = [
            pltpu.make_async_copy(source, target, sems.at[number])
            for number, (source, target) in enumerate(pairs)
        ]
        for copy in copies:
            copy.start()
        earlier = lax.broadcasted_iota(jnp.int32, (local, local), 0)
        later = lax.broadcasted_iota(jnp.int32, (local, local), 1)
        upto = jnp.where(earlier <= later, 1.0, 0.0).astype(BF16)
        expert = lax.broadcasted_iota(jnp.int32, (experts, local), 0)
        copies[0].wait()
        route = route_here[...]
        choose = jnp.where(expert == route, 1.0, 0.0)
        running = dot(choose.astype(BF16), upto, ((1,), (0,)))
        rank = jnp.sum(running * choose, axis=0, keepdims=True) - 1.0
        slot_ref[...] = (route ^ device_ref[0]) * capacity + rank.astype(jnp.int32)
        copies[1].wait()
        factor = column(gate_here[...].reshape(1, local))
        for copy in copies[2:]:
            copy.wait()
        scaled_out[...] = (factor * cotangent_here[...].astype(F32)).astype(BF16)

    def far(array):
        return pltpu.with_memory_space_constraint(array, pltpu.HBM)

    return pl.pallas_call(
        body,
        out_shape=[shape(1, local, jnp.int32), shape(local, width), shape(local, width)],
        in_specs=[pl.BlockSpec(memory_space=pltpu.SMEM)]
        + [pl.BlockSpec(memory_space=pltpu.HBM)] * 4,
        out_specs=[pl.BlockSpec(memory_space=pltpu.VMEM)] * 3,
        scratch_shapes=[
            pltpu.VMEM((1, local), jnp.int32),
            pltpu.VMEM((local,), F32),
            pltpu.VMEM((local, width), BF16),
            pltpu.SemaphoreType.DMA((2 + 2 * pieces,)),
        ],
        cost_estimate=LIGHT,
        compiler_params=pltpu.CompilerParams(vmem_limit_bytes=VMEM_LIMIT),
    )(device, far(route_row), far(gate), far(tokens), far(cotangent))


def dispatch(slots, arrays, blocks, rows, hand_on=False, after=(), weight=HEAVY):
    local, width = arrays[0].shape
    several = len(arrays)

    def body(slot_ref, *refs):
        values, outs = refs[:several], refs[several:]
        number = lax.broadcasted_iota(jnp.int32, (blocks * rows, local), 0)
        placing = jnp.where(number == slot_ref[...], 1.0, 0.0).astype(BF16)
        for which in range(several):
            placed = dot(placing, values[which][...], ((1,), (0,))).astype(BF16)
            for block in range(blocks):
                outs[block][which * rows : (which + 1) * rows, :] = placed[
                    block * rows : (block + 1) * rows
                ]
        if hand_on:
            outs[blocks][...] = slot_ref[...]

    shapes = [shape(several * rows, width)] * blocks + [shape(1, local, jnp.int32)] * hand_on
    return call(body, shapes, slots, *arrays, after=after, weight=weight)


def handed_on(array, after):
    def body(array_ref, out):
        out[...] = array_ref[...]

    return call(body, shape(*array.shape), array, after=after)


def picked(slot_row, refs, base, rows):
    wanted = column(slot_row.astype(F32)).astype(jnp.int32)
    number = lax.broadcasted_iota(jnp.int32, (slot_row.shape[1], len(refs) * rows), 1)
    picking = jnp.where(number == wanted, 1.0, 0.0).astype(BF16)
    every = jnp.concatenate([ref[base : base + rows, :] for ref in refs], axis=0)
    return dot(picking, every, ((1,), (0,)))


def collect(slots, parts, after=()):
    blocks = len(parts)
    rows, width = parts[0].shape

    def body(slot_ref, *refs):
        refs[blocks][...] = picked(slot_ref[...], refs[:blocks], 0, rows).astype(BF16)

    return call(body, shape(slots.shape[1], width), slots, *parts, after=after)


def collect_own(slots, parts, other_out, gate, after=()):
    blocks = len(parts)
    rows, width = parts[0].shape[0] // 2, parts[0].shape[1]
    local = slots.shape[1]

    def body(slot_ref, *refs):
        parts, (other_ref, gate_ref, mixed_ref, back_ref) = refs[:blocks], refs[blocks:]
        out = picked(slot_ref[...], parts, 0, rows) + other_ref[...].astype(F32)
        mixed_ref[...] = (column(gate_ref[...].reshape(1, local)) * out.astype(BF16).astype(F32)).astype(BF16)
        back_ref[...] = picked(slot_ref[...], parts, rows, rows).astype(BF16)

    return call(
        body,
        [shape(local, width)] * 2,
        slots,
        *parts,
        other_out,
        gate,
        after=after,
        space=pltpu.HBM,
    )


def rows_of(refs, which, capacity, base=0):
    start = base + which * capacity
    return jnp.concatenate([ref[start : start + capacity, :] for ref in refs], axis=0)


def put_rows(refs, which, capacity, base, result):
    start = base + which * capacity
    for block, ref in enumerate(refs):
        ref[start : start + capacity, :] = result[block * capacity : (block + 1) * capacity]


def activation(preact):
    square = preact * preact
    tangent = jnp.tanh(0.7978845608 * (preact + 0.044715 * preact * square))
    hidden = 0.5 * preact * (1.0 + tangent)
    slope = 0.5 * (1.0 + tangent) + 0.5 * preact * (1.0 - tangent * tangent) * (
        0.7978845608 * (1.0 + 0.134145 * square)
    )
    return hidden.astype(BF16), slope


def forward(parts, ups, downs, capacity, after=()):
    blocks = len(parts)
    width, half = ups[0].shape
    count = blocks * capacity

    def body(*refs):
        tokens, refs = refs[:blocks], refs[blocks:]
        up, down, refs = refs[:2], refs[2:4], refs[4:]
        outs, hiddens, slopes = refs[:blocks], refs[blocks : blocks + 2], refs[blocks + 2 :]
        for which in range(2):
            preact = dot(rows_of(tokens, which, capacity), up[which][...], ((1,), (0,)))
            hidden, slope = activation(preact)
            hiddens[which][...] = hidden
            slopes[which][...] = slope.astype(BF16)
            result = dot(hidden, down[which][...], ((1,), (0,))).astype(BF16)
            put_rows(outs, which, capacity, 0, result)

    shapes = [shape(2 * capacity, width)] * blocks + [shape(count, half)] * 4
    results = call(body, shapes, *parts, *ups, *downs, after=after)
    return results[:blocks], results[blocks : blocks + 2], results[blocks + 2 :]


def backward(parts, slopes, ups, downs, capacity, after=()):
    blocks = len(parts)
    width, half = ups[0].shape
    count = blocks * capacity

    def body(*refs):
        grads, refs = refs[:blocks], refs[blocks:]
        slope, up, down, refs = refs[:2], refs[2:4], refs[4:6], refs[6:]
        outs, hidden_grads = refs[:blocks], refs[blocks:]
        for which in range(2):
            through = dot(rows_of(grads, which, capacity), down[which][...], ((1,), (1,)))
            hidden_grad = (through * slope[which][...].astype(F32)).astype(BF16)
            hidden_grads[which][...] = hidden_grad
            result = dot(hidden_grad, up[which][...], ((1,), (1,))).astype(BF16)
            put_rows(outs, which, capacity, 0, result)

    shapes = [shape(2 * capacity, width)] * blocks + [shape(count, half)] * 2
    results = call(body, shapes, *parts, *slopes, *ups, *downs, after=after)
    return results[:blocks], results[blocks:]


def both_ways(parts, ups, downs, capacity, after=()):
    blocks = len(parts)
    width, half = ups[0].shape
    count = blocks * capacity
    base = 2 * capacity

    def body(*refs):
        parts, refs = refs[:blocks], refs[blocks:]
        up, down, refs = refs[:2], refs[2:4], refs[4:]
        outs, hiddens, hidden_grads = refs[:blocks], refs[blocks : blocks + 2], refs[blocks + 2 :]
        for which in range(2):
            preact = dot(rows_of(parts, which, capacity), up[which][...], ((1,), (0,)))
            hidden, slope = activation(preact)
            hiddens[which][...] = hidden
            result = dot(hidden, down[which][...], ((1,), (0,))).astype(BF16)
            put_rows(outs, which, capacity, 0, result)
            through = dot(rows_of(parts, which, capacity, base), down[which][...], ((1,), (1,)))
            hidden_grad = (through * slope).astype(BF16)
            hidden_grads[which][...] = hidden_grad
            result = dot(hidden_grad, up[which][...], ((1,), (1,))).astype(BF16)
            put_rows(outs, which, capacity, base, result)

    shapes = [shape(2 * base, width)] * blocks + [shape(count, half)] * 4
    results = call(body, shapes, *parts, *ups, *downs, after=after)
    return results[:blocks], results[blocks : blocks + 2], results[blocks + 2 :]


def panels(array, size):
    return [array[:, start : start + size] for start in range(0, array.shape[1], size)]


def weight_gradients(which, own, pair_x, pair_c, hiddens, hidden_grads, capacity, dtype, after=()):
    blocks = len(pair_x)
    width = pair_x[0].shape[1]
    half = hiddens[0].shape[1]
    size = math.gcd(width, half)

    def body(*refs):
        own, refs = refs[:blocks], refs[blocks:]
        tokens, grads, refs = refs[:blocks], refs[blocks : 2 * blocks], refs[2 * blocks :]
        groups = len(hiddens)
        hidden, hidden_grad, out = refs[:groups], refs[groups:-1], refs[-1]
        both = [jnp.concatenate([ref[...] for ref in pair], axis=0) for pair in (hidden, hidden_grad)]
        rows = [rows_of(own, which, capacity), rows_of(tokens, which, capacity)]
        up = dot(jnp.concatenate(rows, axis=0), both[1], ((0,), (0,)))
        rows = [rows_of(own, which, capacity, 2 * capacity), rows_of(grads, which, capacity)]
        down = dot(both[0], jnp.concatenate(rows, axis=0), ((0,), (0,)))
        start = 0
        for result in (up, down):
            for panel in panels(result, size):
                out[start : start + panel.shape[0], :] = panel.astype(dtype)
                start += panel.shape[0]

    shapes = shape(2 * width * half // size, size, dtype)
    return call(body, shapes, *own, *pair_x, *pair_c, *hiddens, *hidden_grads, after=after)


def joined(terms, peer, width, half, after=()):
    size = terms.shape[1]

    def body(term_ref, peer_ref, up_ref, down_ref):
        start = 0
        for out in (up_ref, down_ref):
            for place in range(out.shape[1] // size):
                stop = start + out.shape[0]
                total = term_ref[start:stop, :] + peer_ref[start:stop, :].astype(F32)
                out[:, place * size : (place + 1) * size] = total.astype(BF16)
                start = stop

    return call(body, [shape(width, half), shape(half, width)], terms, peer, after=after)


def spread_from(parts, first):
    return [
        exchange(part, "expert", 2 * m) if m else part for m, part in enumerate(parts, first)
    ]


def spread(parts):
    return spread_from(parts, 0)


def shards(tokens, gate_prob, routing, up_weight, down_weight, cotangent):
    experts = lax.axis_size("expert")
    opposite = lax.axis_size("section") // 2
    local = tokens.shape[0]
    capacity = -(-2 * local // experts // 16) * 16
    blocks = experts // 2
    device = lax.axis_index("expert").astype(jnp.int32).reshape(1)

    def across(array):
        return exchange(array, "section", opposite)

    rows = 2 * capacity
    pair_tokens = across(tokens)
    ups = (up_weight[0], exchange(up_weight[0], "expert", 1))
    downs = (down_weight[0], exchange(down_weight[0], "expert", 1))

    slots, tokens, scaled = prepare(
        device, routing.reshape(1, local), gate_prob, tokens, cotangent, blocks, capacity
    )
    *sent, own_slots = dispatch(
        slots, (tokens, scaled), blocks, rows, True, after=(ups[1], downs[1]), weight=LIGHT
    )
    own = spread(sent)
    pair_slots = across(own_slots)
    scaled = handed_on(scaled, (pair_tokens, pair_slots))
    pair_scaled = across(scaled)
    sent = dispatch(pair_slots, (pair_tokens,), blocks, rows, after=(scaled,))
    pair_x = spread(sent)
    own_sent, own_hidden, own_hidden_grad = both_ways(own, ups, downs, capacity, after=(sent[0],))
    half = blocks // 2

    def in_two(step, arrays, after):
        first = step(0, arrays[:half], after)
        second = step(1, arrays[half:], (first[0][0],))
        return [spread_from(first[0], 0) + spread_from(second[0], half), first[1:], second[1:]]

    back, *ahead = in_two(
        lambda _, parts, after: forward(parts, ups, downs, capacity, after=after),
        pair_x,
        (own_sent[0],),
    )
    sent = dispatch(pair_slots, (pair_scaled,), blocks, rows, after=(ahead[1][0][0],))
    pair_c = spread(sent)
    term = collect(pair_slots, back, after=(sent[0],))
    other_out = across(term)
    back, *behind = in_two(
        lambda part, parts, after: backward(parts, ahead[part][1], ups, downs, capacity, after=after),
        pair_c,
        (term,),
    )

    def gradients(which, dtype, after):
        return weight_gradients(
            which,
            own,
            pair_x,
            pair_c,
            (own_hidden[which], ahead[0][0][which], ahead[1][0][which]),
            (own_hidden_grad[which], behind[0][0][which], behind[1][0][which]),
            capacity,
            dtype,
            after,
        )

    term = collect(pair_slots, back, after=(other_out,))
    other_back = across(term)
    own_back = spread(own_sent)
    give = gradients(1, BF16, (term,))
    keep = gradients(0, F32, (give,))
    peer = exchange(give, "expert", 1)
    grad_up, grad_down = joined(keep, peer, *ups[0].shape)
    mixed, own_term = collect_own(slots, own_back, other_out, gate_prob, after=(pltpu.with_memory_space_constraint(grad_up, pltpu.HBM),))
    token_grad = (own_term.astype(F32) + other_back.astype(F32)).astype(BF16)
    return (mixed, token_grad, grad_up[None], grad_down[None])


def solution(mesh):
    in_specs = (
        P(("section", "expert"), None),
        P(("section", "expert")),
        P(("section", "expert"), None),
        P(("section", "expert"), None, None),
        P(("section", "expert"), None, None),
        P(("section", "expert"), None),
    )
    out_specs = (
        P(("section", "expert"), None),
        P(("section", "expert"), None),
        P(("section", "expert"), None, None),
        P(("section", "expert"), None, None),
    )
    return jax.shard_map(shards, mesh=mesh, in_specs=in_specs, out_specs=out_specs, check_vma=False)
```

```python
import math

import jax
import jax.numpy as jnp
from jax import lax
from jax.experimental import pallas as pl
from jax.experimental.pallas import tpu as pltpu
from jax.sharding import PartitionSpec as P

F32 = jnp.float32
BF16 = jnp.bfloat16
VMEM_LIMIT = 48 * 1024 * 1024
HEAVY = pl.CostEstimate(flops=30 * 10**9, bytes_accessed=1, transcendentals=0)
LIGHT = pl.CostEstimate(flops=1, bytes_accessed=1, transcendentals=0)


def exchange(array, axis, flip):
    return lax.ppermute(array, axis, [(i, i ^ flip) for i in range(lax.axis_size(axis))])


def dot(a, b, contract):
    return lax.dot_general(a, b, (contract, ((), ())), preferred_element_type=F32)


def call(body, out_shape, *args, after=(), space=pl.ANY, weight=HEAVY):
    waits = len(after)

    def kernel(*refs):
        body(*refs[waits:])

    return pl.pallas_call(
        kernel,
        out_shape=out_shape,
        in_specs=[pl.BlockSpec(memory_space=space)] * waits
        + [pl.BlockSpec(memory_space=pltpu.VMEM)] * len(args),
        cost_estimate=weight,
        compiler_params=pltpu.CompilerParams(vmem_limit_bytes=VMEM_LIMIT),
    )(*after, *args)


def column(row):
    count = row.shape[1]
    down = lax.broadcasted_iota(jnp.int32, (count, count), 0)
    along = lax.broadcasted_iota(jnp.int32, (count, count), 1)
    return jnp.sum(jnp.where(down == along, row, 0.0), axis=1, keepdims=True)


def shape(rows, columns, dtype=BF16):
    return jax.ShapeDtypeStruct((rows, columns), dtype)


def prepare(device, route_row, gate, tokens, cotangent, blocks, capacity):
    local, width = tokens.shape
    experts = 2 * blocks
    pieces = 4
    piece = local // pieces
    parts = [pl.ds(number * piece, piece) for number in range(pieces)]

    def body(device_ref, route_ref, gate_ref, token_ref, cotangent_ref, *refs):
        slot_ref, token_out, scaled_out, route_here, gate_here, cotangent_here, sems = refs
        pairs = [(route_ref, route_here), (gate_ref, gate_here)]
        pairs += [(cotangent_ref.at[part], cotangent_here.at[part]) for part in parts]
        pairs += [(token_ref.at[part], token_out.at[part]) for part in parts]
        copies = [
            pltpu.make_async_copy(source, target, sems.at[number])
            for number, (source, target) in enumerate(pairs)
        ]
        for copy in copies:
            copy.start()
        earlier = lax.broadcasted_iota(jnp.int32, (local, local), 0)
        later = lax.broadcasted_iota(jnp.int32, (local, local), 1)
        upto = jnp.where(earlier <= later, 1.0, 0.0).astype(BF16)
        expert = lax.broadcasted_iota(jnp.int32, (experts, local), 0)
        copies[0].wait()
        route = route_here[...]
        choose = jnp.where(expert == route, 1.0, 0.0)
        running = dot(choose.astype(BF16), upto, ((1,), (0,)))
        rank = jnp.sum(running * choose, axis=0, keepdims=True) - 1.0
        slot_ref[...] = (route ^ device_ref[0]) * capacity + rank.astype(jnp.int32)
        copies[1].wait()
        factor = column(gate_here[...].reshape(1, local))
        for copy in copies[2:]:
            copy.wait()
        scaled_out[...] = (factor * cotangent_here[...].astype(F32)).astype(BF16)

    def far(array):
        return pltpu.with_memory_space_constraint(array, pltpu.HBM)

    return pl.pallas_call(
        body,
        out_shape=[shape(1, local, jnp.int32), shape(local, width), shape(local, width)],
        in_specs=[pl.BlockSpec(memory_space=pltpu.SMEM)]
        + [pl.BlockSpec(memory_space=pltpu.HBM)] * 4,
        out_specs=[pl.BlockSpec(memory_space=pltpu.VMEM)] * 3,
        scratch_shapes=[
            pltpu.VMEM((1, local), jnp.int32),
            pltpu.VMEM((local,), F32),
            pltpu.VMEM((local, width), BF16),
            pltpu.SemaphoreType.DMA((2 + 2 * pieces,)),
        ],
        cost_estimate=LIGHT,
        compiler_params=pltpu.CompilerParams(vmem_limit_bytes=VMEM_LIMIT),
    )(device, far(route_row), far(gate), far(tokens), far(cotangent))


def dispatch(slots, arrays, blocks, rows, hand_on=False, after=(), weight=HEAVY):
    local, width = arrays[0].shape
    several = len(arrays)

    def body(slot_ref, *refs):
        values, outs = refs[:several], refs[several:]
        number = lax.broadcasted_iota(jnp.int32, (blocks * rows, local), 0)
        placing = jnp.where(number == slot_ref[...], 1.0, 0.0).astype(BF16)
        for which in range(several):
            placed = dot(placing, values[which][...], ((1,), (0,))).astype(BF16)
            for block in range(blocks):
                outs[block][which * rows : (which + 1) * rows, :] = placed[
                    block * rows : (block + 1) * rows
                ]
        if hand_on:
            outs[blocks][...] = slot_ref[...]

    shapes = [shape(several * rows, width)] * blocks + [shape(1, local, jnp.int32)] * hand_on
    return call(body, shapes, slots, *arrays, after=after, weight=weight)


def handed_on(array, after):
    def body(array_ref, out):
        out[...] = array_ref[...]

    return call(body, shape(*array.shape, array.dtype), array, after=after)


def picked(slot_row, refs, base, rows):
    wanted = column(slot_row.astype(F32)).astype(jnp.int32)
    number = lax.broadcasted_iota(jnp.int32, (slot_row.shape[1], len(refs) * rows), 1)
    picking = jnp.where(number == wanted, 1.0, 0.0).astype(BF16)
    every = jnp.concatenate([ref[base : base + rows, :] for ref in refs], axis=0)
    return dot(picking, every, ((1,), (0,)))


def collect(slots, parts, after=()):
    blocks = len(parts)
    rows, width = parts[0].shape

    def body(slot_ref, *refs):
        refs[blocks][...] = picked(slot_ref[...], refs[:blocks], 0, rows).astype(BF16)

    return call(body, shape(slots.shape[1], width), slots, *parts, after=after)


def collect_own(slots, parts, other_out, gate, after=()):
    blocks = len(parts)
    rows, width = parts[0].shape[0] // 2, parts[0].shape[1]
    local = slots.shape[1]

    def body(slot_ref, *refs):
        parts, (other_ref, gate_ref, mixed_ref, back_ref) = refs[:blocks], refs[blocks:]
        out = picked(slot_ref[...], parts, 0, rows) + other_ref[...].astype(F32)
        mixed_ref[...] = (column(gate_ref[...].reshape(1, local)) * out.astype(BF16).astype(F32)).astype(BF16)
        back_ref[...] = picked(slot_ref[...], parts, rows, rows).astype(BF16)

    return call(
        body,
        [shape(local, width)] * 2,
        slots,
        *parts,
        other_out,
        gate,
        after=after,
        space=pltpu.HBM,
    )


def rows_of(refs, which, capacity, base=0):
    start = base + which * capacity
    return jnp.concatenate([ref[start : start + capacity, :] for ref in refs], axis=0)


def put_rows(refs, which, capacity, base, result):
    start = base + which * capacity
    for block, ref in enumerate(refs):
        ref[start : start + capacity, :] = result[block * capacity : (block + 1) * capacity]


def activation(preact):
    square = preact * preact
    tangent = jnp.tanh(0.7978845608 * (preact + 0.044715 * preact * square))
    hidden = 0.5 * preact * (1.0 + tangent)
    slope = 0.5 * (1.0 + tangent) + 0.5 * preact * (1.0 - tangent * tangent) * (
        0.7978845608 * (1.0 + 0.134145 * square)
    )
    return hidden.astype(BF16), slope


def forward(parts, ups, downs, capacity, after=()):
    blocks = len(parts)
    width, half = ups[0].shape
    count = blocks * capacity

    def body(*refs):
        tokens, refs = refs[:blocks], refs[blocks:]
        up, down, refs = refs[:2], refs[2:4], refs[4:]
        outs, hiddens, slopes = refs[:blocks], refs[blocks : blocks + 2], refs[blocks + 2 :]
        for which in range(2):
            preact = dot(rows_of(tokens, which, capacity), up[which][...], ((1,), (0,)))
            hidden, slope = activation(preact)
            hiddens[which][...] = hidden
            slopes[which][...] = slope.astype(BF16)
            result = dot(hidden, down[which][...], ((1,), (0,))).astype(BF16)
            put_rows(outs, which, capacity, 0, result)

    shapes = [shape(2 * capacity, width)] * blocks + [shape(count, half)] * 4
    results = call(body, shapes, *parts, *ups, *downs, after=after)
    return results[:blocks], results[blocks : blocks + 2], results[blocks + 2 :]


def backward(parts, slopes, ups, downs, capacity, after=()):
    blocks = len(parts)
    width, half = ups[0].shape
    count = blocks * capacity

    def body(*refs):
        grads, refs = refs[:blocks], refs[blocks:]
        slope, up, down, refs = refs[:2], refs[2:4], refs[4:6], refs[6:]
        outs, hidden_grads = refs[:blocks], refs[blocks:]
        for which in range(2):
            through = dot(rows_of(grads, which, capacity), down[which][...], ((1,), (1,)))
            hidden_grad = (through * slope[which][...].astype(F32)).astype(BF16)
            hidden_grads[which][...] = hidden_grad
            result = dot(hidden_grad, up[which][...], ((1,), (1,))).astype(BF16)
            put_rows(outs, which, capacity, 0, result)

    shapes = [shape(2 * capacity, width)] * blocks + [shape(count, half)] * 2
    results = call(body, shapes, *parts, *slopes, *ups, *downs, after=after)
    return results[:blocks], results[blocks:]


def both_ways(parts, ups, downs, capacity, after=()):
    blocks = len(parts)
    width, half = ups[0].shape
    count = blocks * capacity
    base = 2 * capacity

    def body(*refs):
        parts, refs = refs[:blocks], refs[blocks:]
        up, down, refs = refs[:2], refs[2:4], refs[4:]
        outs, hiddens, hidden_grads = refs[:blocks], refs[blocks : blocks + 2], refs[blocks + 2 :]
        for which in range(2):
            preact = dot(rows_of(parts, which, capacity), up[which][...], ((1,), (0,)))
            hidden, slope = activation(preact)
            hiddens[which][...] = hidden
            result = dot(hidden, down[which][...], ((1,), (0,))).astype(BF16)
            put_rows(outs, which, capacity, 0, result)
            through = dot(rows_of(parts, which, capacity, base), down[which][...], ((1,), (1,)))
            hidden_grad = (through * slope).astype(BF16)
            hidden_grads[which][...] = hidden_grad
            result = dot(hidden_grad, up[which][...], ((1,), (1,))).astype(BF16)
            put_rows(outs, which, capacity, base, result)

    shapes = [shape(2 * base, width)] * blocks + [shape(count, half)] * 4
    results = call(body, shapes, *parts, *ups, *downs, after=after)
    return results[:blocks], results[blocks : blocks + 2], results[blocks + 2 :]


def panels(array, size):
    return [array[:, start : start + size] for start in range(0, array.shape[1], size)]


def weight_gradients(which, own, pair_x, pair_c, hiddens, hidden_grads, capacity, dtype, after=()):
    blocks = len(pair_x)
    width = pair_x[0].shape[1]
    half = hiddens[0].shape[1]
    size = math.gcd(width, half)

    def body(*refs):
        own, refs = refs[:blocks], refs[blocks:]
        tokens, grads, refs = refs[:blocks], refs[blocks : 2 * blocks], refs[2 * blocks :]
        groups = len(hiddens)
        hidden, hidden_grad, out = refs[:groups], refs[groups:-1], refs[-1]
        both = [jnp.concatenate([ref[...] for ref in pair], axis=0) for pair in (hidden, hidden_grad)]
        rows = [rows_of(own, which, capacity), rows_of(tokens, which, capacity)]
        up = dot(jnp.concatenate(rows, axis=0), both[1], ((0,), (0,)))
        rows = [rows_of(own, which, capacity, 2 * capacity), rows_of(grads, which, capacity)]
        down = dot(both[0], jnp.concatenate(rows, axis=0), ((0,), (0,)))
        start = 0
        for result in (up, down):
            for panel in panels(result, size):
                out[start : start + panel.shape[0], :] = panel.astype(dtype)
                start += panel.shape[0]

    shapes = shape(2 * width * half // size, size, dtype)
    return call(body, shapes, *own, *pair_x, *pair_c, *hiddens, *hidden_grads, after=after)


def joined(terms, peer, width, half, after=()):
    size = terms.shape[1]

    def body(term_ref, peer_ref, up_ref, down_ref):
        start = 0
        for out in (up_ref, down_ref):
            for place in range(out.shape[1] // size):
                stop = start + out.shape[0]
                total = term_ref[start:stop, :] + peer_ref[start:stop, :].astype(F32)
                out[:, place * size : (place + 1) * size] = total.astype(BF16)
                start = stop

    return call(body, [shape(width, half), shape(half, width)], terms, peer, after=after)


def spread_from(parts, first):
    return [
        exchange(part, "expert", 2 * m) if m else part for m, part in enumerate(parts, first)
    ]


def spread(parts):
    return spread_from(parts, 0)


def shards(tokens, gate_prob, routing, up_weight, down_weight, cotangent):
    experts = lax.axis_size("expert")
    opposite = lax.axis_size("section") // 2
    local = tokens.shape[0]
    capacity = -(-2 * local // experts // 16) * 16
    blocks = experts // 2
    device = lax.axis_index("expert").astype(jnp.int32).reshape(1)

    def across(array):
        return exchange(array, "section", opposite)

    rows = 2 * capacity
    pair_tokens = across(tokens)
    ups = (up_weight[0], exchange(up_weight[0], "expert", 1))
    downs = (down_weight[0], exchange(down_weight[0], "expert", 1))

    slots, tokens, scaled = prepare(
        device, routing.reshape(1, local), gate_prob, tokens, cotangent, blocks, capacity
    )
    *sent, own_slots = dispatch(
        slots, (tokens, scaled), blocks, rows, True, weight=LIGHT
    )
    own = spread(sent)
    own_slots = handed_on(own_slots, (ups[1], downs[1]))
    pair_slots = across(own_slots)
    scaled = handed_on(scaled, (pair_tokens, pair_slots))
    pair_scaled = across(scaled)
    sent = dispatch(pair_slots, (pair_tokens,), blocks, rows, after=(scaled,))
    pair_x = spread(sent)
    own_sent, own_hidden, own_hidden_grad = both_ways(own, ups, downs, capacity, after=(sent[0],))
    half = blocks // 2

    def in_two(step, arrays, after):
        first = step(0, arrays[:half], after)
        second = step(1, arrays[half:], (first[0][0],))
        return [spread_from(first[0], 0) + spread_from(second[0], half), first[1:], second[1:]]

    back, *ahead = in_two(
        lambda _, parts, after: forward(parts, ups, downs, capacity, after=after),
        pair_x,
        (own_sent[0],),
    )
    sent = dispatch(pair_slots, (pair_scaled,), blocks, rows, after=(ahead[1][0][0],))
    pair_c = spread(sent)
    term = collect(pair_slots, back, after=(sent[0],))
    other_out = across(term)
    back, *behind = in_two(
        lambda part, parts, after: backward(parts, ahead[part][1], ups, downs, capacity, after=after),
        pair_c,
        (term,),
    )

    def gradients(which, dtype, after):
        return weight_gradients(
            which,
            own,
            pair_x,
            pair_c,
            (own_hidden[which], ahead[0][0][which], ahead[1][0][which]),
            (own_hidden_grad[which], behind[0][0][which], behind[1][0][which]),
            capacity,
            dtype,
            after,
        )

    term = collect(pair_slots, back, after=(other_out,))
    other_back = across(term)
    own_back = spread(own_sent)
    give = gradients(1, BF16, (term,))
    keep = gradients(0, F32, (give,))
    peer = exchange(give, "expert", 1)
    grad_up, grad_down = joined(keep, peer, *ups[0].shape)
    mixed, own_term = collect_own(slots, own_back, other_out, gate_prob, after=(pltpu.with_memory_space_constraint(grad_up, pltpu.HBM),))
    token_grad = (own_term.astype(F32) + other_back.astype(F32)).astype(BF16)
    return (mixed, token_grad, grad_up[None], grad_down[None])


def solution(mesh):
    in_specs = (
        P(("section", "expert"), None),
        P(("section", "expert")),
        P(("section", "expert"), None),
        P(("section", "expert"), None, None),
        P(("section", "expert"), None, None),
        P(("section", "expert"), None),
    )
    out_specs = (
        P(("section", "expert"), None),
        P(("section", "expert"), None),
        P(("section", "expert"), None, None),
        P(("section", "expert"), None, None),
    )
    return jax.shard_map(shards, mesh=mesh, in_specs=in_specs, out_specs=out_specs, check_vma=False)
```

```python
import math

import jax
import jax.numpy as jnp
from jax import lax
from jax.experimental import pallas as pl
from jax.experimental.pallas import tpu as pltpu
from jax.sharding import PartitionSpec as P

F32 = jnp.float32
BF16 = jnp.bfloat16
VMEM_LIMIT = 48 * 1024 * 1024
HEAVY = pl.CostEstimate(flops=30 * 10**9, bytes_accessed=1, transcendentals=0)
LIGHT = pl.CostEstimate(flops=1, bytes_accessed=1, transcendentals=0)


def exchange(array, axis, flip):
    return lax.ppermute(array, axis, [(i, i ^ flip) for i in range(lax.axis_size(axis))])


def dot(a, b, contract):
    return lax.dot_general(a, b, (contract, ((), ())), preferred_element_type=F32)


def call(body, out_shape, *args, after=(), space=pl.ANY, weight=HEAVY):
    waits = len(after)

    def kernel(*refs):
        body(*refs[waits:])

    return pl.pallas_call(
        kernel,
        out_shape=out_shape,
        in_specs=[pl.BlockSpec(memory_space=space)] * waits
        + [pl.BlockSpec(memory_space=pltpu.VMEM)] * len(args),
        cost_estimate=weight,
        compiler_params=pltpu.CompilerParams(vmem_limit_bytes=VMEM_LIMIT),
    )(*after, *args)


def column(row):
    count = row.shape[1]
    down = lax.broadcasted_iota(jnp.int32, (count, count), 0)
    along = lax.broadcasted_iota(jnp.int32, (count, count), 1)
    return jnp.sum(jnp.where(down == along, row, 0.0), axis=1, keepdims=True)


def shape(rows, columns, dtype=BF16):
    return jax.ShapeDtypeStruct((rows, columns), dtype)


def prepare(device, route_row, gate, tokens, cotangent, blocks, capacity):
    local, width = tokens.shape
    experts = 2 * blocks
    pieces = 4
    piece = local // pieces
    parts = [pl.ds(number * piece, piece) for number in range(pieces)]

    def body(device_ref, route_ref, gate_ref, token_ref, cotangent_ref, *refs):
        slot_ref, token_out, scaled_out, route_here, gate_here, cotangent_here, sems = refs
        pairs = [(route_ref, route_here), (gate_ref, gate_here)]
        pairs += [(cotangent_ref.at[part], cotangent_here.at[part]) for part in parts]
        pairs += [(token_ref.at[part], token_out.at[part]) for part in parts]
        copies = [
            pltpu.make_async_copy(source, target, sems.at[number])
            for number, (source, target) in enumerate(pairs)
        ]
        for copy in copies:
            copy.start()
        earlier = lax.broadcasted_iota(jnp.int32, (local, local), 0)
        later = lax.broadcasted_iota(jnp.int32, (local, local), 1)
        upto = jnp.where(earlier <= later, 1.0, 0.0).astype(BF16)
        expert = lax.broadcasted_iota(jnp.int32, (experts, local), 0)
        copies[0].wait()
        route = route_here[...]
        choose = jnp.where(expert == route, 1.0, 0.0)
        running = dot(choose.astype(BF16), upto, ((1,), (0,)))
        rank = jnp.sum(running * choose, axis=0, keepdims=True) - 1.0
        slot_ref[...] = (route ^ device_ref[0]) * capacity + rank.astype(jnp.int32)
        copies[1].wait()
        factor = column(gate_here[...].reshape(1, local))
        for copy in copies[2:]:
            copy.wait()
        scaled_out[...] = (factor * cotangent_here[...].astype(F32)).astype(BF16)

    def far(array):
        return pltpu.with_memory_space_constraint(array, pltpu.HBM)

    return pl.pallas_call(
        body,
        out_shape=[shape(1, local, jnp.int32), shape(local, width), shape(local, width)],
        in_specs=[pl.BlockSpec(memory_space=pltpu.SMEM)]
        + [pl.BlockSpec(memory_space=pltpu.HBM)] * 4,
        out_specs=[pl.BlockSpec(memory_space=pltpu.VMEM)] * 3,
        scratch_shapes=[
            pltpu.VMEM((1, local), jnp.int32),
            pltpu.VMEM((local,), F32),
            pltpu.VMEM((local, width), BF16),
            pltpu.SemaphoreType.DMA((2 + 2 * pieces,)),
        ],
        cost_estimate=LIGHT,
        compiler_params=pltpu.CompilerParams(vmem_limit_bytes=VMEM_LIMIT),
    )(device, far(route_row), far(gate), far(tokens), far(cotangent))


def dispatch(slots, arrays, blocks, rows, hand_on=False, after=(), weight=HEAVY):
    local, width = arrays[0].shape
    several = len(arrays)

    def body(slot_ref, *refs):
        values, outs = refs[:several], refs[several:]
        number = lax.broadcasted_iota(jnp.int32, (blocks * rows, local), 0)
        placing = jnp.where(number == slot_ref[...], 1.0, 0.0).astype(BF16)
        for which in range(several):
            placed = dot(placing, values[which][...], ((1,), (0,))).astype(BF16)
            for block in range(blocks):
                outs[block][which * rows : (which + 1) * rows, :] = placed[
                    block * rows : (block + 1) * rows
                ]
        if hand_on:
            outs[blocks][...] = slot_ref[...]

    shapes = [shape(several * rows, width)] * blocks + [shape(1, local, jnp.int32)] * hand_on
    return call(body, shapes, slots, *arrays, after=after, weight=weight)


def handed_on(array, after):
    def body(array_ref, out):
        out[...] = array_ref[...]

    return call(body, shape(*array.shape, array.dtype), array, after=after)


def picked(slot_row, refs, base, rows):
    wanted = column(slot_row.astype(F32)).astype(jnp.int32)
    number = lax.broadcasted_iota(jnp.int32, (slot_row.shape[1], len(refs) * rows), 1)
    picking = jnp.where(number == wanted, 1.0, 0.0).astype(BF16)
    every = jnp.concatenate([ref[base : base + rows, :] for ref in refs], axis=0)
    return dot(picking, every, ((1,), (0,)))


def collect(slots, parts, after=()):
    blocks = len(parts)
    rows, width = parts[0].shape

    def body(slot_ref, *refs):
        refs[blocks][...] = picked(slot_ref[...], refs[:blocks], 0, rows).astype(BF16)

    return call(body, shape(slots.shape[1], width), slots, *parts, after=after)


def collect_own(slots, parts, other_out, gate, after=()):
    blocks = len(parts)
    rows, width = parts[0].shape[0] // 2, parts[0].shape[1]
    local = slots.shape[1]

    def body(slot_ref, *refs):
        parts, (other_ref, gate_ref, mixed_ref, back_ref) = refs[:blocks], refs[blocks:]
        out = picked(slot_ref[...], parts, 0, rows) + other_ref[...].astype(F32)
        factor = column(gate_ref[...].reshape(1, local))
        mixed_ref[...] = (factor * out.astype(BF16).astype(F32)).astype(BF16)
        back_ref[...] = picked(slot_ref[...], parts, rows, rows).astype(BF16)

    kept = [pltpu.VMEM((local, width), BF16)] * 2
    return call(body, kept, slots, *parts, other_out, gate, after=after, space=pltpu.HBM)


def finished(mixed, one, other):
    local, width = mixed.shape
    pieces = 4
    piece = local // pieces
    parts = [pl.ds(number * piece, piece) for number in range(pieces)]

    def body(mixed_ref, one_ref, other_ref, mixed_out, sum_out, here, sems):
        copies = [
            pltpu.make_async_copy(source.at[part], target.at[part], sems.at[index, number])
            for index, (source, target) in enumerate(((mixed_ref, mixed_out), (here, sum_out)))
            for number, part in enumerate(parts)
        ]
        for copy in copies[:pieces]:
            copy.start()
        for part, copy in zip(parts, copies[pieces:]):
            total = one_ref[part, :].astype(F32) + other_ref[part, :].astype(F32)
            here[part, :] = total.astype(BF16)
            copy.start()
        for copy in copies:
            copy.wait()

    return pl.pallas_call(
        body,
        out_shape=[shape(local, width)] * 2,
        out_specs=[pl.BlockSpec(memory_space=pl.ANY)] * 2,
        scratch_shapes=[pltpu.VMEM((local, width), BF16), pltpu.SemaphoreType.DMA((2, pieces))],
        cost_estimate=HEAVY,
        compiler_params=pltpu.CompilerParams(vmem_limit_bytes=VMEM_LIMIT),
    )(mixed, one, other)


def rows_of(refs, which, capacity, base=0):
    start = base + which * capacity
    return jnp.concatenate([ref[start : start + capacity, :] for ref in refs], axis=0)


def put_rows(refs, which, capacity, base, result):
    start = base + which * capacity
    for block, ref in enumerate(refs):
        ref[start : start + capacity, :] = result[block * capacity : (block + 1) * capacity]


def activation(preact):
    square = preact * preact
    tangent = jnp.tanh(0.7978845608 * (preact + 0.044715 * preact * square))
    hidden = 0.5 * preact * (1.0 + tangent)
    slope = 0.5 * (1.0 + tangent) + 0.5 * preact * (1.0 - tangent * tangent) * (
        0.7978845608 * (1.0 + 0.134145 * square)
    )
    return hidden.astype(BF16), slope


def forward(parts, ups, downs, capacity, after=()):
    blocks = len(parts)
    width, half = ups[0].shape
    count = blocks * capacity

    def body(*refs):
        tokens, refs = refs[:blocks], refs[blocks:]
        up, down, refs = refs[:2], refs[2:4], refs[4:]
        outs, hiddens, slopes = refs[:blocks], refs[blocks : blocks + 2], refs[blocks + 2 :]
        for which in range(2):
            preact = dot(rows_of(tokens, which, capacity), up[which][...], ((1,), (0,)))
            hidden, slope = activation(preact)
            hiddens[which][...] = hidden
            slopes[which][...] = slope.astype(BF16)
            result = dot(hidden, down[which][...], ((1,), (0,))).astype(BF16)
            put_rows(outs, which, capacity, 0, result)

    shapes = [shape(2 * capacity, width)] * blocks + [shape(count, half)] * 4
    results = call(body, shapes, *parts, *ups, *downs, after=after)
    return results[:blocks], results[blocks : blocks + 2], results[blocks + 2 :]


def backward(parts, slopes, ups, downs, capacity, after=()):
    blocks = len(parts)
    width, half = ups[0].shape
    count = blocks * capacity

    def body(*refs):
        grads, refs = refs[:blocks], refs[blocks:]
        slope, up, down, refs = refs[:2], refs[2:4], refs[4:6], refs[6:]
        outs, hidden_grads = refs[:blocks], refs[blocks:]
        for which in range(2):
            through = dot(rows_of(grads, which, capacity), down[which][...], ((1,), (1,)))
            hidden_grad = (through * slope[which][...].astype(F32)).astype(BF16)
            hidden_grads[which][...] = hidden_grad
            result = dot(hidden_grad, up[which][...], ((1,), (1,))).astype(BF16)
            put_rows(outs, which, capacity, 0, result)

    shapes = [shape(2 * capacity, width)] * blocks + [shape(count, half)] * 2
    results = call(body, shapes, *parts, *slopes, *ups, *downs, after=after)
    return results[:blocks], results[blocks:]


def both_ways(parts, ups, downs, capacity, after=()):
    blocks = len(parts)
    width, half = ups[0].shape
    count = blocks * capacity
    base = 2 * capacity

    def body(*refs):
        parts, refs = refs[:blocks], refs[blocks:]
        up, down, refs = refs[:2], refs[2:4], refs[4:]
        outs, hiddens, hidden_grads = refs[:blocks], refs[blocks : blocks + 2], refs[blocks + 2 :]
        for which in range(2):
            preact = dot(rows_of(parts, which, capacity), up[which][...], ((1,), (0,)))
            hidden, slope = activation(preact)
            hiddens[which][...] = hidden
            result = dot(hidden, down[which][...], ((1,), (0,))).astype(BF16)
            put_rows(outs, which, capacity, 0, result)
            through = dot(rows_of(parts, which, capacity, base), down[which][...], ((1,), (1,)))
            hidden_grad = (through * slope).astype(BF16)
            hidden_grads[which][...] = hidden_grad
            result = dot(hidden_grad, up[which][...], ((1,), (1,))).astype(BF16)
            put_rows(outs, which, capacity, base, result)

    shapes = [shape(2 * base, width)] * blocks + [shape(count, half)] * 4
    results = call(body, shapes, *parts, *ups, *downs, after=after)
    return results[:blocks], results[blocks : blocks + 2], results[blocks + 2 :]


def panels(array, size):
    return [array[:, start : start + size] for start in range(0, array.shape[1], size)]


def weight_gradients(which, own, pair_x, pair_c, hiddens, hidden_grads, capacity, dtype, after=()):
    blocks = len(pair_x)
    width = pair_x[0].shape[1]
    half = hiddens[0].shape[1]
    size = math.gcd(width, half)

    def body(*refs):
        own, refs = refs[:blocks], refs[blocks:]
        tokens, grads, refs = refs[:blocks], refs[blocks : 2 * blocks], refs[2 * blocks :]
        groups = len(hiddens)
        hidden, hidden_grad, out = refs[:groups], refs[groups:-1], refs[-1]
        both = [jnp.concatenate([ref[...] for ref in pair], axis=0) for pair in (hidden, hidden_grad)]
        rows = [rows_of(own, which, capacity), rows_of(tokens, which, capacity)]
        up = dot(jnp.concatenate(rows, axis=0), both[1], ((0,), (0,)))
        rows = [rows_of(own, which, capacity, 2 * capacity), rows_of(grads, which, capacity)]
        down = dot(both[0], jnp.concatenate(rows, axis=0), ((0,), (0,)))
        start = 0
        for result in (up, down):
            for panel in panels(result, size):
                out[start : start + panel.shape[0], :] = panel.astype(dtype)
                start += panel.shape[0]

    shapes = shape(2 * width * half // size, size, dtype)
    return call(body, shapes, *own, *pair_x, *pair_c, *hiddens, *hidden_grads, after=after)


def joined(terms, peer, width, half, after=()):
    size = terms.shape[1]

    def body(term_ref, peer_ref, up_ref, down_ref):
        start = 0
        for out in (up_ref, down_ref):
            for place in range(out.shape[1] // size):
                stop = start + out.shape[0]
                total = term_ref[start:stop, :] + peer_ref[start:stop, :].astype(F32)
                out[:, place * size : (place + 1) * size] = total.astype(BF16)
                start = stop

    return call(body, [shape(width, half), shape(half, width)], terms, peer, after=after)


def spread_from(parts, first):
    return [
        exchange(part, "expert", 2 * m) if m else part for m, part in enumerate(parts, first)
    ]


def spread(parts):
    return spread_from(parts, 0)


def shards(tokens, gate_prob, routing, up_weight, down_weight, cotangent):
    experts = lax.axis_size("expert")
    opposite = lax.axis_size("section") // 2
    local = tokens.shape[0]
    capacity = -(-2 * local // experts // 16) * 16
    blocks = experts // 2
    device = lax.axis_index("expert").astype(jnp.int32).reshape(1)

    def across(array):
        return exchange(array, "section", opposite)

    rows = 2 * capacity
    pair_tokens = across(tokens)
    ups = (up_weight[0], exchange(up_weight[0], "expert", 1))
    downs = (down_weight[0], exchange(down_weight[0], "expert", 1))

    slots, tokens, scaled = prepare(
        device, routing.reshape(1, local), gate_prob, tokens, cotangent, blocks, capacity
    )
    *sent, own_slots = dispatch(
        slots, (tokens, scaled), blocks, rows, True, weight=LIGHT
    )
    own = spread(sent)
    own_slots = handed_on(own_slots, (ups[1], downs[1]))
    pair_slots = across(own_slots)
    scaled = handed_on(scaled, (pair_tokens, pair_slots))
    pair_scaled = across(scaled)
    sent = dispatch(pair_slots, (pair_tokens,), blocks, rows, after=(scaled,), weight=LIGHT)
    pair_x = spread(sent)
    own_sent, own_hidden, own_hidden_grad = both_ways(own, ups, downs, capacity, after=(sent[0],))
    half = blocks // 2

    def in_two(step, arrays, after):
        first = step(0, arrays[:half], after)
        second = step(1, arrays[half:], (first[0][0],))
        return [spread_from(first[0], 0) + spread_from(second[0], half), first[1:], second[1:]]

    back, *ahead = in_two(
        lambda _, parts, after: forward(parts, ups, downs, capacity, after=after),
        pair_x,
        (own_sent[0],),
    )
    sent = dispatch(pair_slots, (pair_scaled,), blocks, rows, after=(ahead[1][0][0],))
    pair_c = spread(sent)
    term = collect(pair_slots, back, after=(sent[0],))
    other_out = across(term)
    back, *behind = in_two(
        lambda part, parts, after: backward(parts, ahead[part][1], ups, downs, capacity, after=after),
        pair_c,
        (term,),
    )

    def gradients(which, dtype, after):
        return weight_gradients(
            which,
            own,
            pair_x,
            pair_c,
            (own_hidden[which], ahead[0][0][which], ahead[1][0][which]),
            (own_hidden_grad[which], behind[0][0][which], behind[1][0][which]),
            capacity,
            dtype,
            after,
        )

    term = collect(pair_slots, back, after=(other_out,))
    other_back = across(term)
    own_back = spread(own_sent)
    give = gradients(1, BF16, (term,))
    keep = gradients(0, F32, (give,))
    peer = exchange(give, "expert", 1)
    grad_up, grad_down = joined(keep, peer, *ups[0].shape)
    mixed, own_term = collect_own(slots, own_back, other_out, gate_prob, after=(pltpu.with_memory_space_constraint(grad_up, pltpu.HBM),))
    mixed, token_grad = finished(mixed, own_term, other_back)
    return (mixed, token_grad, grad_up[None], grad_down[None])


def solution(mesh):
    in_specs = (
        P(("section", "expert"), None),
        P(("section", "expert")),
        P(("section", "expert"), None),
        P(("section", "expert"), None, None),
        P(("section", "expert"), None, None),
        P(("section", "expert"), None),
    )
    out_specs = (
        P(("section", "expert"), None),
        P(("section", "expert"), None),
        P(("section", "expert"), None, None),
        P(("section", "expert"), None, None),
    )
    return jax.shard_map(shards, mesh=mesh, in_specs=in_specs, out_specs=out_specs, check_vma=False)
```
